512 devices in a mesh: slab: 64 (over z_lo, x, core), head: 8 (over y, z_hi).
Axes of the slice: x: 4, y: 4, z: 16 (z_hi: 2, z_lo: 8; z = z_hi * 8 + z_lo), core: 2. Of those that a mesh axis runs over, the one named last changes fastest.
Arguments:
- tokens: bfloat16 [64, 64, 16, 768], P('slab', 'head'), may hold values from -60 to 60
- cotangent: bfloat16 [64, 64, 16, 768], P('slab', 'head'), may hold values from -16 to 16
- weights: bfloat16 [768, 4, 512], P('slab', None, 'head'), may hold values from -2 to 2
- norm_gain: float32 [768], replicated, may hold values from 0.5 to 1.5
- norm_bias: float32 [768], replicated, may hold values from -3 to 3
Outputs:
- grad_tokens: bfloat16 [64, 64, 16, 768], P('slab', 'head')
- grad_weights: float32 [768, 4, 512], P('slab', None, 'head')
- grad_norm: float32 [2, 768], replicated
The draws below stay inside these ranges and needn't reach their ends.
All inputs are finite; a program needn't handle non-finite values.
Results may differ from the reference program's by a relative error of at most 0.011.
Values may be sent and summed in bfloat16 or wider, within the bound.
A program may use at most 64 MiB of HBM per device.

```python
import math
import jax
import jax.numpy as jnp
from jax import lax

D = 768
HD = 64
HEADS = 8
NX = 64
NY = 16
HH = 512
NZ = 64


def draw_tokens(key, part):
    key = jax.random.fold_in(key, 11)
    key_one, key_two, key_three = jax.random.split(key, 3)
    feature_scale = jnp.exp(jax.random.uniform(key_two, (D,), jnp.float32, 0.0, math.log(10.0)))
    token_scale = jnp.exp(jax.random.uniform(key_three, (NZ, NX, NY, 1), jnp.float32, 0.0, math.log(2.0)))
    raw_draw = jnp.clip(jax.random.normal(key_one, (NZ, NX, NY, D), jnp.float32), -3.0, 3.0)
    values = raw_draw * feature_scale * token_scale
    return jnp.clip(values, -60.0, 60.0).astype(jnp.bfloat16)


def draw_weights(key, part):
    key = jax.random.fold_in(key, 23)
    raw_draw = jnp.clip(jax.random.normal(key, (D, 4, HH), jnp.float32), -4.0, 4.0)
    component = jnp.arange(4)
    fan_scale = jnp.where(component == 3, HH ** (-0.5), D ** (-0.5)).astype(jnp.float32)
    values = raw_draw * fan_scale[None, :, None]
    return jnp.clip(values, -2.0, 2.0).astype(jnp.bfloat16)


def strengthened(values, stream_key, source, target, parts, factor):
    owner, partner = [(jnp.arange(values.shape[dim]) // (values.shape[dim] // parts)).reshape([-1 if axis == dim else 1 for axis in range(values.ndim)]) for dim in (source, target)]
    chosen = jax.random.permutation(stream_key, parts)[partner]
    strong = (owner == chosen) | (owner == (partner + parts // 2) % parts)
    return jnp.where(strong, factor * values, values)


def block_scale(own_key, shape, shards, smallest, high):
    loudness, own = 1.0, jax.random.fold_in(own_key, 6)
    for dim, shards_of in shards:
        draws = jnp.exp(jax.random.uniform(jax.random.fold_in(own, dim), (shards_of,), jnp.float32, smallest / len(shards), high / len(shards)))
        loudness = loudness * jnp.repeat(draws, shape[dim] // shards_of).reshape([-1 if axis == dim else 1 for axis in range(len(shape))])
    return loudness


def noise(stream_key, shape, scale, reach, cuts=(), held_as=jnp.bfloat16):
    values = jax.random.normal(stream_key, shape, jnp.float32) * scale
    if len(cuts) > 0:
        values = block_scale(stream_key, shape, cuts, -0.22, 0.18) * values
    return jnp.clip(values, min=-reach, max=reach).astype(held_as)


def gaussian_with(stream_key, extent, width, reach, pieces, heavy, held_as=jnp.bfloat16):
    entries = width * jax.random.normal(stream_key, extent, jnp.float32)
    if pieces:
        entries = entries * block_scale(stream_key, extent, pieces, -0.22, 0.18)
    return jnp.clip(strengthened(entries, jax.random.fold_in(stream_key, 3), *heavy), -reach, reach).astype(held_as)


def setup_inputs(seed: int = 0) -> dict:
    seeds = jax.random.split(jax.random.key(seed), 6)
    return {
        "tokens": draw_tokens(jax.random.fold_in(seeds[5], 71), 0),
        "cotangent": gaussian_with(seeds[1], (NZ, NX, NY, D), 1.0, 16.0, ((0, 64), (1, 8)), (0, 3, 64, 4.0)),
        "weights": draw_weights(jax.random.fold_in(seeds[5], 71), 0),
        "norm_gain": jnp.clip(1.0 + 0.1 * jax.random.normal(seeds[3], (D,), jnp.float32), 0.5, 1.5),
        "norm_bias": noise(seeds[4], (D,), 0.5, 3.0, (), jnp.float32),
    }


def line_grads(q_lines, k_lines, v_lines, u_lines):
    score_scale = 1.0 / q_lines.shape[-1] ** 0.5
    q_full = q_lines.astype(jnp.float32)
    k_full = k_lines.astype(jnp.float32)
    v_full = v_lines.astype(jnp.float32)
    u_full = u_lines.astype(jnp.float32)
    scores = jnp.einsum('bld,bmd->blm', q_full, k_full) * score_scale
    probs_f = jax.nn.softmax(scores, axis=-1)
    probs_low = probs_f.astype(jnp.bfloat16).astype(jnp.float32)
    output = jnp.einsum('blm,bmd->bld', probs_low, v_full).astype(jnp.bfloat16)
    dprobs = jnp.einsum('bld,bmd->blm', u_full, v_full)
    delta = lax.optimization_barrier(jnp.sum(probs_f * dprobs, axis=-1, keepdims=True))
    dscores = (probs_f * (dprobs - delta) * score_scale).astype(jnp.bfloat16).astype(jnp.float32)
    grad_q = jnp.einsum('blm,bmd->bld', dscores, k_full).astype(jnp.bfloat16)
    grad_k = jnp.einsum('blm,bld->bmd', dscores, q_full).astype(jnp.bfloat16)
    grad_v = jnp.einsum('blm,bld->bmd', probs_low, u_full).astype(jnp.bfloat16)
    return (output, grad_q, grad_k, grad_v)

def axis_lines(inputs, axis_order, inverse):
    first = inputs[0]
    moved_shape = tuple((first.shape[i] for i in axis_order))
    moved = [jnp.transpose(tensor, axis_order).reshape(-1, moved_shape[2], moved_shape[3]) for tensor in inputs]
    results = line_grads(*moved)
    return [jnp.transpose(tensor.reshape(moved_shape), inverse) for tensor in results]

def head_grads(inputs):
    along_x = axis_lines(inputs, (0, 2, 1, 3), (0, 2, 1, 3))
    along_y = axis_lines(inputs, (0, 1, 2, 3), (0, 1, 2, 3))
    along_z = axis_lines(inputs, (1, 2, 0, 3), (2, 0, 1, 3))
    return tuple(((one.astype(jnp.float32) + two.astype(jnp.float32) + three.astype(jnp.float32)).astype(jnp.bfloat16) for one, two, three in zip(along_x, along_y, along_z)))

def reference(tokens, cotangent, weights, norm_gain, norm_bias):
    tok_rows = tokens.astype(jnp.float32).reshape(-1, D)
    tok_mean = lax.optimization_barrier(jnp.mean(tok_rows, axis=-1, keepdims=True))
    centred = tok_rows - tok_mean
    inv_std = lax.rsqrt(lax.optimization_barrier(jnp.mean(centred * centred, axis=-1, keepdims=True)) + 1e-05)
    normalised = centred * inv_std
    normed = (normalised * norm_gain + norm_bias).astype(jnp.bfloat16)
    flat_c = cotangent.reshape(-1, D)
    qkv_weights = weights[:, :3].reshape(D, 3 * HH)
    projected = jnp.dot(normed, qkv_weights, preferred_element_type=jnp.float32).astype(jnp.bfloat16)
    projected = projected.reshape(NZ, NX, NY, 3, HEADS, HD)
    upstream = jnp.dot(flat_c, weights[:, 3], preferred_element_type=jnp.float32).astype(jnp.bfloat16)
    upstream = upstream.reshape(NZ, NX, NY, HEADS, HD)
    stacked = (jnp.moveaxis(projected[:, :, :, 0], 3, 0), jnp.moveaxis(projected[:, :, :, 1], 3, 0), jnp.moveaxis(projected[:, :, :, 2], 3, 0), jnp.moveaxis(upstream, 3, 0))
    head_out = lax.map(head_grads, stacked)
    flat_out = [jnp.moveaxis(tensor, 0, 3).reshape(-1, HH) for tensor in head_out]
    attended = flat_out[0]
    grads_qkv = jnp.stack(flat_out[1:], axis=1).reshape(-1, 3 * HH)
    grad_normed = jnp.dot(grads_qkv, qkv_weights.T, preferred_element_type=jnp.float32)
    qkv_part = jnp.dot(normed.T, grads_qkv, preferred_element_type=jnp.float32).reshape(D, 3, HH)
    out_part = jnp.dot(flat_c.T, attended, preferred_element_type=jnp.float32)
    grad_weights = jnp.concatenate([qkv_part, out_part[:, None, :]], axis=1)
    gain_sum = lax.optimization_barrier(jnp.sum(grad_normed * normalised, axis=0))
    bias_sum = lax.optimization_barrier(jnp.sum(grad_normed, axis=0))
    grad_norm = jnp.stack([gain_sum, bias_sum])
    scaled = grad_normed * norm_gain
    mean_g = lax.optimization_barrier(jnp.mean(scaled, axis=-1, keepdims=True))
    mean_gx = lax.optimization_barrier(jnp.mean(scaled * normalised, axis=-1, keepdims=True))
    grad_rows = flat_c.astype(jnp.float32) + inv_std * (scaled - mean_g - normalised * mean_gx)
    grad_tokens = grad_rows.astype(jnp.bfloat16).reshape(NZ, NX, NY, D)
    return (grad_tokens, grad_weights, grad_norm)
```

```python
import jax
import jax.numpy as jnp
from jax import lax
from jax.experimental import pallas as pl
from jax.experimental.pallas import tpu as pltpu
from jax.sharding import PartitionSpec as P

MESH = pl.DeviceIdType.MESH
BF = jnp.bfloat16
F32 = jnp.float32
EPS = 1e-05
SCALE = 0.125


def one_hot(rows, cols, source):
    dest = lax.broadcasted_iota(jnp.int32, (rows, cols), 0)
    src = lax.broadcasted_iota(jnp.int32, (rows, cols), 1)
    return (source(dest) == src).astype(BF)


def dot(a, b):
    return jnp.dot(a, b, preferred_element_type=F32)


def dot_nt(a, b):
    return lax.dot_general(a, b, (((1,), (1,)), ((), ())), preferred_element_type=F32)


def dot_tn(a, b):
    return lax.dot_general(a, b, (((0,), (0,)), ((), ())), preferred_element_type=F32)


def kernel(
    tok, cot, wpiece, gain, bias,
    out_tok, out_w, out_norm,
    wq, wb_piece, zw, wb,
    send_rows, p1, xb, zv, zb,
    lt, gs, nrm_y, inv_y, gn_acc, gn_y,
    gx, xg, gz, zg, rb, ret,
    gw_send, gw_recv, gw_own, ys, yr, yacc, xs, xr, zs, zr,
    nc, ny_, nx_, nz_,
    s_q, r_q, s_wz, r_wz, s_wx, r_wx, s_wy, r_wy, s_wc, r_wc,
    s_p1, r_p1, s_2a, r_2a, s_2b, r_2b,
    s_gx, r_gx, s_gz, r_gz, s_rt, r_rt,
    s_c, r_c, s_y, r_y, s_x, r_x, s_z, r_z, s_f, r_f,
    s_nc, r_nc, s_ny, r_ny, s_nx, r_nx, s_nz, r_nz,
):
    slab = lax.axis_index("slab")
    head = lax.axis_index("head")
    z_lo, x, core = slab // 8, (slab // 2) % 4, slab % 2
    y, z_hi = head // 2, head % 2
    z = z_hi * 8 + z_lo
    k = x * 2 + core
    xp = x // 2
    member = (x % 2) * 2 + core

    def at_z(c):
        return ((c % 8) * 8 + k, y * 2 + c // 8)

    def at_y(v):
        return (slab, v * 2 + z_hi)

    def at_k(v):
        return (z_lo * 8 + v, head)

    def rcopy(src, dst, ssem, rsem, dev):
        return pltpu.make_async_remote_copy(
            src_ref=src, dst_ref=dst, send_sem=ssem, recv_sem=rsem, device_id=dev, device_id_type=MESH
        )

    def arrived(dst, rsem, ssem, dev):
        rcopy(dst, dst, ssem, rsem, dev).wait_recv()

    barrier = pltpu.get_barrier_semaphore()

    @pl.loop(1, 16)
    def _(d):
        pl.semaphore_signal(barrier, inc=1, device_id=at_z((z + d) % 16), device_id_type=MESH)

    for d in range(1, 4):
        pl.semaphore_signal(barrier, inc=1, device_id=at_y((y + d) % 4), device_id_type=MESH)
    for d in range(1, 8):
        pl.semaphore_signal(barrier, inc=1, device_id=at_k((k + d) % 8), device_id_type=MESH)
    pl.semaphore_wait(barrier, 25)

    wq[member] = wpiece[...]
    sends = []

    def go(copy):
        copy.start()
        sends.append(copy)

    def quad(d):
        other = (member + d) % 4
        return other, at_k(((x // 2) * 2 + other // 2) * 2 + other % 2)

    for d in range(1, 4):
        other, dev = quad(d)
        go(rcopy(wq.at[member], wq.at[member], s_q.at[d], r_q.at[member], dev))

    perm = one_hot(128, 128, lambda i: (i % 8) * 16 + i // 8)
    t_rows = dot(perm, tok[...])
    c_rows = dot(perm, cot[...])
    send_rows[...] = jnp.concatenate(
        [t_rows.reshape(16, 8, 768), c_rows.reshape(16, 8, 768)], axis=1
    ).astype(BF)

    for d in range(1, 4):
        other, dev = quad(d)
        arrived(wq.at[other], r_q.at[other], s_q.at[d], dev)
    stack = one_hot(48, 64, lambda i: (i // 12) * 16 + i % 12)
    block = dot(stack, wq[...].reshape(64, 256)).astype(BF)
    wb_piece[0] = block[:, :128]
    wb_piece[1] = block[:, 128:]
    zw[z_lo, z_hi] = wb_piece[core]

    @pl.loop(1, 16)
    def _(d):
        c = (z + d) % 16
        rcopy(wb_piece.at[core], zw.at[z_lo, z_hi], s_wz.at[d], r_wz.at[z], at_z(c)).start()

    p1[z_lo, z_hi] = send_rows[z]

    @pl.loop(1, 16)
    def _(d):
        c = (z + d) % 16
        rcopy(send_rows.at[c], p1.at[z_lo, z_hi], s_p1.at[d], r_p1.at[z], at_z(c)).start()

    @pl.loop(1, 16)
    def _(d):
        c = (z + d) % 16
        arrived(zw.at[c % 8, c // 8], r_wz.at[c], s_wz.at[d], at_z(c))

    for c2 in range(2):
        merged = sum(
            dot(
                zw[:, zh].reshape(384, 128),
                lane_map(c2, zh),
            )
            for zh in range(2)
        )
        wb[core, y, c2, :, xp] = merged.astype(BF).reshape(8, 48, 128)
    mate = (3 - x) * 2 + core
    go(rcopy(wb.at[core, y, :, :, xp], wb.at[core, y, :, :, xp], s_wx, r_wx, at_k(mate)))
    arrived(wb.at[core, y, :, :, 1 - xp], r_wx, s_wx, at_k(mate))
    for d in range(1, 4):
        go(rcopy(wb.at[core, y], wb.at[core, y], s_wy.at[d], r_wy.at[y], at_y((y + d) % 4)))
    pair = at_k(x * 2 + 1 - core)
    go(rcopy(wb.at[core, y], wb.at[core, y], s_wc.at[0], r_wc.at[y], pair))

    @pl.loop(1, 16)
    def _(d):
        c = (z + d) % 16
        arrived(p1.at[c % 8, c // 8], r_p1.at[c], s_p1.at[d], at_z(c))

    for d in range(1, 4):
        v = (y + d) % 4
        go(rcopy(p1.at[pl.ds(2 * v, 2)], xb.at[:, y], s_2a.at[d], r_2a.at[y], at_y(v)))
    xb[:, y] = p1[pl.ds(2 * y, 2)]
    perm_v = one_hot(
        256, 256, lambda i: (i % 8) * 32 + (i // 128) * 16 + ((i // 8) % 2) * 8 + (i // 16) % 8
    )
    zv[...] = dot(perm_v, p1[...].reshape(256, 768)).astype(BF).reshape(8, 2, 16, 768)
    for d in range(1, 8):
        v = (k + d) % 8
        go(rcopy(zv.at[v], zb.at[:, k], s_2b.at[d], r_2b.at[k], at_k(v)))
    zb[:, k] = zv[k]

    for d in (1, 3, 2):
        v = (y + d) % 4
        arrived(wb.at[core, v], r_wy.at[v], s_wy.at[d], at_y(v))
        go(rcopy(wb.at[core, v], wb.at[core, v], s_wc.at[d], r_wc.at[v], pair))
    for d in range(4):
        v = (y + d) % 4
        arrived(wb.at[1 - core, v], r_wc.at[v], s_wc.at[d], pair)

    gain_row, bias_row = gain[...], bias[...]
    row_i = lax.broadcasted_iota(jnp.int32, (128, 128), 0)
    col_i = lax.broadcasted_iota(jnp.int32, (128, 128), 1)

    def home(idx, rows, same):
        f = rows.astype(F32)
        t = f[:, :8].reshape(128, 768)
        c16 = f[:, 8:].reshape(128, 768).astype(BF)
        centred = t - jnp.mean(t, axis=-1, keepdims=True)
        inv = lax.rsqrt(jnp.mean(centred * centred, axis=-1, keepdims=True) + EPS)
        nrm = centred * inv
        normed = (nrm * gain_row + bias_row).astype(BF)
        lt[0, :, idx * 128:(idx + 1) * 128] = normed.T
        lt[1, :, idx * 128:(idx + 1) * 128] = c16.T
        gn_acc[...] = jnp.zeros_like(gn_acc)

        @pl.loop(0, 2)
        def _(hq):
            def w_of(c):
                parts = [wb[c // 2, 2 * hq + e, c % 2].reshape(768, 128) for e in range(2)]
                return jnp.concatenate(parts, axis=1)

            q = dot(normed, w_of(0)).astype(BF)
            kk = dot(normed, w_of(1)).astype(BF)
            v = dot(normed, w_of(2)).astype(BF)
            u = dot(c16, w_of(3)).astype(BF)
            lane_head = lax.broadcasted_iota(jnp.int32, (128, 256), 1) // 64

            def spread(a):
                return jnp.concatenate(
                    [jnp.where(lane_head == j, a, jnp.zeros_like(a)) for j in range(4)], axis=0
                )

            qs, ks, vs, us = spread(q), spread(kk), spread(v), spread(u)
            s = dot_nt(q, ks)
            dp = dot_nt(u, vs)
            lows, dss = [], []
            for j in range(4):
                sj = jnp.where(same, s[:, j * 128:(j + 1) * 128] * SCALE, -1e30)
                e = jnp.exp(sj - jnp.max(sj, axis=-1, keepdims=True))
                pr = e / jnp.sum(e, axis=-1, keepdims=True)
                dpj = dp[:, j * 128:(j + 1) * 128]
                delta = jnp.sum(pr * dpj, axis=-1, keepdims=True)
                dss.append((pr * (dpj - delta) * SCALE).astype(BF))
                lows.append(pr.astype(BF))
            p_wide, ds_wide = jnp.concatenate(lows, axis=1), jnp.concatenate(dss, axis=1)
            p_tall, ds_tall = jnp.concatenate(lows, axis=0), jnp.concatenate(dss, axis=0)
            att = dot(p_wide, vs).astype(BF)
            gq = dot(ds_wide, ks).astype(BF)
            gk = dot_tn(ds_tall, qs).astype(BF)
            gv = dot_tn(p_tall, us).astype(BF)
            for c, g in enumerate((gq, gk, gv, att)):
                gs[c, hq, idx * 128:(idx + 1) * 128, :] = g
            gn_acc[...] += dot_nt(gq, w_of(0)) + dot_nt(gk, w_of(1)) + dot_nt(gv, w_of(2))

        g = gn_acc[...]
        part = jnp.concatenate(
            [jnp.sum(g * nrm, axis=0, keepdims=True), jnp.sum(g, axis=0, keepdims=True)], axis=0
        )
        return g, nrm, inv, part

    g, nrm, inv, norm_part = home(0, send_rows[...], row_i % 8 == col_i % 8)
    gn_y[...] = g
    nrm_y[...] = nrm
    inv_y[...] = jnp.broadcast_to(inv, (128, 128))

    for d in range(1, 4):
        v = (y + d) % 4
        arrived(xb.at[:, v], r_2a.at[v], s_2a.at[d], at_y(v))
    half = row_i // 64 == col_i // 64
    g, _, _, part = home(1, xb[...].reshape(16, 16, 768), half)
    norm_part = norm_part + part
    gx[...] = g.astype(BF).reshape(2, 4, 16, 768)
    for d in range(1, 4):
        v = (y + d) % 4
        go(rcopy(gx.at[:, v], xg.at[pl.ds(2 * y, 2)], s_gx.at[d], r_gx.at[y], at_y(v)))
    xg[pl.ds(2 * y, 2)] = gx[:, y]

    for d in range(1, 8):
        v = (k + d) % 8
        arrived(zb.at[:, v], r_2b.at[v], s_2b.at[d], at_k(v))
    g, _, _, part = home(2, zb[...].reshape(16, 16, 768), half)
    norm_part = norm_part + part
    g4 = g.reshape(2, 8, 8, 768)
    gz[...] = jnp.concatenate([g4[0], g4[1]], axis=1).astype(BF)
    for d in range(1, 8):
        v = (k + d) % 8
        go(rcopy(gz.at[v], zg.at[k], s_gz.at[d], r_gz.at[k], at_k(v)))
    zg[k] = gz[k]

    nc[core] = norm_part
    go(rcopy(nc.at[core], nc.at[core], s_nc, r_nc, pair))

    def weight_grad(c, hq):
        return dot(lt[jnp.where(c == 3, 1, 0)], gs[c, hq])

    for hq in range(2):
        for c2 in range(2):
            full = weight_grad(2 * (1 - core) + c2, hq).astype(BF)
            gw_send[2 * hq, c2] = full[:, :128]
            gw_send[2 * hq + 1, c2] = full[:, 128:]
        for e in range(2):
            v = 2 * hq + e
            go(rcopy(gw_send.at[v], gw_recv.at[v], s_c.at[v], r_c.at[v], pair))
    for hq in range(2):
        for c2 in range(2):
            full = weight_grad(2 * core + c2, hq)
            gw_own[2 * hq, c2] = full[:, :128]
            gw_own[2 * hq + 1, c2] = full[:, 128:]

    for d in range(1, 4):
        v = (y + d) % 4
        arrived(xg.at[pl.ds(2 * v, 2)], r_gx.at[v], s_gx.at[d], at_y(v))
    for d in range(1, 8):
        v = (k + d) % 8
        arrived(zg.at[v], r_gz.at[v], s_gz.at[d], at_k(v))
    perm_g = one_hot(128, 128, lambda i: (i % 16) * 8 + i // 16)
    total = dot(perm_g, zg[...].reshape(128, 768)) + xg[...].reshape(128, 768).astype(F32)
    total = total.reshape(16, 8, 768)
    rb[...] = jnp.concatenate([total[:, :, :384], total[:, :, 384:]], axis=1).astype(BF)

    @pl.loop(1, 16)
    def _(d):
        c = (z + d) % 16
        rcopy(rb.at[(c % 8) * 2 + c // 8], ret.at[z], s_rt.at[d], r_rt.at[z], at_z(c)).start()

    ret[z] = rb[z_lo * 2 + z_hi]

    for d in (2, 1, 3, 0):
        v = (y + d) % 4
        arrived(gw_recv.at[v], r_c.at[v], s_c.at[v], pair)
        ys[v] = (gw_own[v] + gw_recv[v].astype(F32)).astype(BF)
        if d:
            go(rcopy(ys.at[v], yr.at[y], s_y.at[d], r_y.at[y], at_y(v)))
    yr[y] = ys[y]
    arrived(nc.at[1 - core], r_nc, s_nc, pair)
    ny_[y] = nc[0] + nc[1]
    for d in range(1, 4):
        go(rcopy(ny_.at[y], ny_.at[y], s_ny.at[d], r_ny.at[y], at_y((y + d) % 4)))
    for d in range(1, 4):
        v = (y + d) % 4
        arrived(yr.at[v], r_y.at[v], s_y.at[d], at_y(v))
        arrived(ny_.at[v], r_ny.at[v], s_ny.at[d], at_y(v))
    y_total = yr[0].astype(F32) + yr[1].astype(F32) + yr[2].astype(F32) + yr[3].astype(F32)
    yacc[...] = y_total.astype(BF).reshape(2, 8, 2, 48, 128)
    nx_[x] = (ny_[0] + ny_[1]) + (ny_[2] + ny_[3])

    for d in (2, 1, 3, 0):
        v = (x + d) % 4
        xs[v] = yacc[v % 2, :, v // 2]
        if d:
            dev = at_k(v * 2 + core)
            go(rcopy(xs.at[v], xr.at[x], s_x.at[d], r_x.at[x], dev))
            go(rcopy(nx_.at[x], nx_.at[x], s_nx.at[d], r_nx.at[x], dev))
    xr[x] = xs[x]
    for d in range(1, 4):
        v = (x + d) % 4
        dev = at_k(v * 2 + core)
        arrived(xr.at[v], r_x.at[v], s_x.at[d], dev)
        arrived(nx_.at[v], r_nx.at[v], s_nx.at[d], dev)
    x_total = xr[0].astype(F32) + xr[1].astype(F32) + xr[2].astype(F32) + xr[3].astype(F32)
    zs[...] = x_total.astype(BF)
    nz_[z] = (nx_[0] + nx_[1]) + (nx_[2] + nx_[3])

    @pl.loop(1, 16)
    def _(d):
        c = (z + d) % 16
        rcopy(zs.at[c % 8], zr.at[z], s_z.at[d], r_z.at[z], at_z(c)).start()
        rcopy(nz_.at[z], nz_.at[z], s_nz.at[d], r_nz.at[z], at_z(c)).start()

    zr[z] = zs[z_lo]

    @pl.loop(1, 16)
    def _(d):
        c = (z + d) % 16
        arrived(ret.at[c], r_rt.at[c], s_rt.at[d], at_z(c))

    back = ret[...].astype(F32)
    back = jnp.concatenate([back[:, :8], back[:, 8:]], axis=2).reshape(128, 768)
    grad_normed = gn_y[...] + back
    scaled = grad_normed * gain_row
    nrm = nrm_y[...]
    m1 = jnp.mean(scaled, axis=-1, keepdims=True)
    m2 = jnp.mean(scaled * nrm, axis=-1, keepdims=True)
    c_rows = send_rows[...].astype(F32)[:, 8:].reshape(128, 768)
    rows = (c_rows + inv_y[:, :1] * (scaled - m1 - nrm * m2)).astype(BF)
    perm_b = one_hot(128, 128, lambda i: (i % 16) * 8 + i // 16)
    out_tok[...] = dot(perm_b, rows).astype(BF)

    @pl.loop(1, 16)
    def _(d):
        c = (z + d) % 16
        arrived(zr.at[c], r_z.at[c], s_z.at[d], at_z(c))
        arrived(nz_.at[c], r_nz.at[c], s_nz.at[d], at_z(c))

    z_total = zr[0].astype(F32)
    norm_total = nz_[0]
    for c in range(1, 16):
        z_total = z_total + zr[c].astype(F32)
        norm_total = norm_total + nz_[c]
    out_norm[...] = norm_total

    mine = 2 * core + x % 2
    out_w[mine] = z_total
    for d in range(1, 4):
        other, dev = quad(d)
        go(rcopy(out_w.at[mine], out_w.at[mine], s_f.at[d], r_f.at[mine], dev))
    for d in range(1, 4):
        other, dev = quad(d)
        theirs = 2 * (other % 2) + other // 2
        arrived(out_w.at[theirs], r_f.at[theirs], s_f.at[d], dev)

    for copy in sends:
        copy.wait_send()

    @pl.loop(1, 16)
    def _(d):
        c = (z + d) % 16
        dev = at_z(c)
        rcopy(wb_piece.at[core], zw.at[z_lo, z_hi], s_wz.at[d], r_wz.at[z], dev).wait_send()
        rcopy(send_rows.at[c], p1.at[z_lo, z_hi], s_p1.at[d], r_p1.at[z], dev).wait_send()
        rcopy(rb.at[(c % 8) * 2 + c // 8], ret.at[z], s_rt.at[d], r_rt.at[z], dev).wait_send()
        rcopy(zs.at[c % 8], zr.at[z], s_z.at[d], r_z.at[z], dev).wait_send()
        rcopy(nz_.at[z], nz_.at[z], s_nz.at[d], r_nz.at[z], dev).wait_send()


def lane_map(c2, zh):
    src = lax.broadcasted_iota(jnp.int32, (128, 128), 0)
    dest = lax.broadcasted_iota(jnp.int32, (128, 128), 1)
    return ((dest // 64 == zh) & (src == c2 * 64 + dest % 64)).astype(BF)


def per_device(tokens, cotangent, weights, norm_gain, norm_bias):
    tok = tokens.reshape(128, 768)
    cot = cotangent.reshape(128, 768)
    piece = jnp.pad(weights.reshape(12, 256), ((0, 4), (0, 0)))
    vm = pltpu.VMEM
    dma = pltpu.SemaphoreType.DMA
    scratch = [
        vm((4, 16, 256), BF),
        vm((2, 48, 128), BF),
        vm((8, 2, 48, 128), BF),
        vm((2, 4, 2, 8, 2, 48, 128), BF),
        vm((16, 16, 768), BF),
        vm((8, 2, 16, 768), BF),
        vm((2, 4, 2, 16, 768), BF),
        vm((8, 2, 16, 768), BF),
        vm((2, 8, 16, 768), BF),
        vm((2, 768, 384), BF),
        vm((4, 2, 384, 256), BF),
        vm((128, 768), F32),
        vm((128, 128), F32),
        vm((128, 768), F32),
        vm((128, 768), F32),
        vm((2, 4, 16, 768), BF),
        vm((8, 16, 768), BF),
        vm((8, 16, 768), BF),
        vm((8, 16, 768), BF),
        vm((16, 16, 384), BF),
        vm((16, 16, 384), BF),
        vm((4, 2, 768, 128), BF),
        vm((4, 2, 768, 128), BF),
        vm((4, 2, 768, 128), F32),
        vm((4, 2, 768, 128), BF),
        vm((4, 2, 768, 128), BF),
        vm((2, 8, 2, 48, 128), BF),
        vm((4, 8, 48, 128), BF),
        vm((4, 8, 48, 128), BF),
        vm((8, 48, 128), BF),
        vm((16, 48, 128), BF),
        vm((2, 2, 768), F32),
        vm((4, 2, 768), F32),
        vm((4, 2, 768), F32),
        vm((16, 2, 768), F32),
        dma((4,)), dma((4,)),
        dma((16,)), dma((16,)),
        dma, dma,
        dma((4,)), dma((4,)),
        dma((4,)), dma((4,)),
        dma((16,)), dma((16,)),
        dma((4,)), dma((4,)),
        dma((8,)), dma((8,)),
        dma((4,)), dma((4,)),
        dma((8,)), dma((8,)),
        dma((16,)), dma((16,)),
        dma((4,)), dma((4,)),
        dma((4,)), dma((4,)),
        dma((4,)), dma((4,)),
        dma((16,)), dma((16,)),
        dma((4,)), dma((4,)),
        dma, dma,
        dma((4,)), dma((4,)),
        dma((4,)), dma((4,)),
        dma((16,)), dma((16,)),
    ]
    whole = pl.BlockSpec(memory_space=pltpu.VMEM)
    grad_tok, grad_w, grad_norm = pl.pallas_call(
        kernel,
        out_shape=(
            jax.ShapeDtypeStruct((128, 768), BF),
            jax.ShapeDtypeStruct((4, 48, 128), F32),
            jax.ShapeDtypeStruct((2, 768), F32),
        ),
        in_specs=[whole] * 5,
        out_specs=(whole, whole, whole),
        scratch_shapes=scratch,
        compiler_params=pltpu.CompilerParams(
            collective_id=0, has_side_effects=True, vmem_limit_bytes=52 * 1024 * 1024
        ),
        name="axial_backward",
    )(tok, cot, piece, norm_gain.reshape(1, 768), norm_bias.reshape(1, 768))
    slab = lax.axis_index("slab")
    head = lax.axis_index("head")
    mine = lax.dynamic_slice(grad_w, (0, (slab % 4) * 12, (head % 2) * 64), (4, 12, 64))
    return grad_tok.reshape(tokens.shape), mine.transpose(1, 0, 2), grad_norm


def solution(mesh):
    return jax.shard_map(
        per_device,
        mesh=mesh,
        in_specs=(
            P("slab", "head", None, None),
            P("slab", "head", None, None),
            P("slab", None, "head"),
            P(),
            P(),
        ),
        out_specs=(P("slab", "head", None, None), P("slab", None, "head"), P()),
        check_vma=False,
    )
```

```python
import types

import jax
import jax.numpy as jnp
from jax import lax
from jax.experimental import pallas as pl
from jax.experimental.pallas import tpu as pltpu
from jax.sharding import PartitionSpec as P

MESH = pl.DeviceIdType.MESH
BF = jnp.bfloat16
F32 = jnp.float32
EPS = 1e-05
SCALE = 0.125
VM = pltpu.VMEM

BUFFERS = {
    "tok": VM((128, 768), BF),
    "cot": VM((128, 768), BF),
    "wraw": VM((12, 4, 64), BF),
    "gain": VM((768,), F32),
    "bias": VM((768,), F32),
    "wq": VM((4, 16, 256), BF),
    "wpart": VM((2, 48, 128), BF),
    "wb": VM((2, 2, 4, 4, 4, 48, 128), BF),
    "send_rows": VM((16, 16, 768), BF),
    "p1": VM((8, 2, 16, 768), BF),
    "xb": VM((2, 4, 2, 16, 768), BF),
    "zv": VM((8, 2, 16, 768), BF),
    "zb": VM((2, 8, 16, 768), BF),
    "lt": VM((2, 768, 384), BF),
    "gs_qk": VM((2, 384, 512), BF),
    "gs_v": VM((2, 384, 256), BF),
    "gs_a": VM((2, 384, 256), BF),
    "nrm_y": VM((128, 768), F32),
    "inv_y": VM((128, 128), F32),
    "gn_acc": VM((128, 768), F32),
    "gn_y": VM((128, 768), F32),
    "gx": VM((2, 4, 16, 768), BF),
    "xg": VM((8, 16, 768), BF),
    "gz": VM((8, 16, 768), BF),
    "zg": VM((8, 16, 768), BF),
    "rb": VM((8, 2, 16, 384), BF),
    "ret": VM((16, 16, 384), BF),
    "gw_send": VM((2, 4, 768, 128), BF),
    "gw_recv": VM((2, 4, 768, 128), BF),
    "gw_own": VM((2, 4, 768, 128), F32),
    "a1s": VM((4, 768, 128), BF),
    "a1r": VM((4, 768, 128), BF),
    "b1s": VM((4, 4, 4, 48, 128), BF),
    "b1r": VM((4, 4, 4, 48, 128), BF),
    "a2s": VM((4, 4, 48, 128), BF),
    "a2r": VM((4, 4, 48, 128), BF),
    "b2s": VM((4, 4, 48, 128), BF),
    "b2r": VM((4, 4, 48, 128), BF),
    "zs": VM((2, 4, 48, 128), BF),
    "zr": VM((16, 48, 128), BF),
    "qr": VM((2, 48, 128), F32),
    "tok_out": VM((128, 768), BF),
    "norm_out": VM((2, 768), F32),
    "nc": VM((2, 2, 768), F32),
    "ny": VM((4, 2, 768), F32),
    "nx": VM((4, 2, 768), F32),
    "nz": VM((16, 2, 768), F32),
}
SEMAPHORES = {
    "q": 4, "wz": 16, "wa1": 4, "wb1": 4, "wa2": 4, "wb2": 4, "wca": 4, "wcb": 4,
    "p1": 16, "xl": 4, "zl": 8, "gx": 4, "gz": 8, "rt": 16,
    "c": 2, "a1": 4, "b1": 4, "a2": 4, "b2": 4, "z": 16, "f": 4,
    "nc": 2, "ny": 4, "nx": 4, "nz": 16,
}


def one_hot(rows, cols, source):
    dest = lax.broadcasted_iota(jnp.int32, (rows, cols), 0)
    src = lax.broadcasted_iota(jnp.int32, (rows, cols), 1)
    return (source(dest) == src).astype(BF)


def dot(a, b):
    return jnp.dot(a, b, preferred_element_type=F32)


def dot_nt(a, b):
    return lax.dot_general(a, b, (((1,), (1,)), ((), ())), preferred_element_type=F32)


def dot_tn(a, b):
    return lax.dot_general(a, b, (((0,), (0,)), ((), ())), preferred_element_type=F32)


def swap(a, b):
    low = lax.broadcasted_iota(jnp.int32, a.shape, 1) < 64
    return jnp.where(low, a, pltpu.roll(b, 64, 1)), jnp.where(low, pltpu.roll(a, 64, 1), b)


def kernel(tok_in, cot_in, w_in, gain_in, bias_in, tok_res, w_res, norm_res, *refs):
    names = list(BUFFERS)
    r = types.SimpleNamespace(**dict(zip(names, refs)))
    rest = refs[len(names):]
    ssem = {n: rest[2 * i] for i, n in enumerate(SEMAPHORES)}
    rsem = {n: rest[2 * i + 1] for i, n in enumerate(SEMAPHORES)}
    lsem = rest[-1]

    slab = lax.axis_index("slab")
    head = lax.axis_index("head")
    z_lo, x, core = slab // 8, (slab // 2) % 4, slab % 2
    y, z_hi = head // 2, head % 2
    z = z_hi * 8 + z_lo
    k = x * 2 + core
    p = x % 2
    j = 2 * p + x // 2
    member = p * 2 + core
    holder = z_lo % 2 == p

    def at_z(c):
        return ((c % 8) * 8 + k, y * 2 + c // 8)

    def at_y(v):
        return (slab, v * 2 + z_hi)

    def at_k(v):
        return (z_lo * 8 + v, head)

    def at_x(v):
        return at_k(v * 2 + core)

    def j_of(v):
        return 2 * (v % 2) + v // 2

    pair = at_k(x * 2 + 1 - core)

    def rcopy(name, src, dst, si, ri, dev):
        return pltpu.make_async_remote_copy(
            src_ref=src, dst_ref=dst, send_sem=ssem[name].at[si], recv_sem=rsem[name].at[ri],
            device_id=dev, device_id_type=MESH,
        )

    sends = []

    def go(*args):
        copy = rcopy(*args)
        copy.start()
        sends.append(copy)

    def arrived(name, dst, ri, dev):
        rcopy(name, dst, dst, 0, ri, dev).wait_recv()

    loads = [
        pltpu.make_async_copy(src, dst, lsem.at[i])
        for i, (src, dst) in enumerate(
            ((w_in, r.wraw), (tok_in, r.tok), (cot_in, r.cot), (gain_in, r.gain), (bias_in, r.bias))
        )
    ]
    for load in loads:
        load.start()

    barrier = pltpu.get_barrier_semaphore()

    @pl.loop(1, 16)
    def _(d):
        pl.semaphore_signal(barrier, inc=1, device_id=at_z((z + d) % 16), device_id_type=MESH)

    for d in range(1, 4):
        pl.semaphore_signal(barrier, inc=1, device_id=at_y((y + d) % 4), device_id_type=MESH)
    for d in range(1, 8):
        pl.semaphore_signal(barrier, inc=1, device_id=at_k((k + d) % 8), device_id_type=MESH)

    loads[0].wait()
    wide = jnp.concatenate([r.wraw[:, c, :].astype(F32) for c in range(4)], axis=1)
    wide = jnp.concatenate([wide, jnp.zeros((4, 256), F32)], axis=0)
    r.wq[member] = wide.astype(BF)
    for load in loads[1:]:
        load.wait()

    perm = one_hot(128, 128, lambda i: (i % 8) * 16 + i // 8)
    t_rows = dot(perm, r.tok[...])
    c_rows = dot(perm, r.cot[...])
    r.send_rows[...] = jnp.concatenate(
        [t_rows.reshape(16, 8, 768), c_rows.reshape(16, 8, 768)], axis=1
    ).astype(BF)

    pl.semaphore_wait(barrier, 25)

    def quad(d):
        other = (member + d) % 4
        return other, at_k(((other // 2) + 2 * (x // 2)) * 2 + other % 2)

    for d in range(1, 4):
        other, dev = quad(d)
        go("q", r.wq.at[member], r.wq.at[member], d, member, dev)
    for d in range(1, 4):
        other, dev = quad(d)
        arrived("q", r.wq.at[other], other, dev)
    stack = one_hot(48, 64, lambda i: (i // 12) * 16 + i % 12)
    block = dot(stack, r.wq[...].reshape(64, 256)).astype(BF)
    r.wpart[0] = block[:, :128]
    r.wpart[1] = block[:, 128:]

    w_mine = r.wb.at[core, z_hi, y, z_lo // 2, j]

    @pl.when(holder)
    def _():
        w_mine[...] = r.wpart[core]

        @pl.loop(1, 16)
        def _(d):
            rcopy("wz", r.wpart.at[core], w_mine, d, z, at_z((z + d) % 16)).start()

    r.p1[z_lo, z_hi] = r.send_rows[z]

    @pl.loop(1, 16)
    def _(d):
        c = (z + d) % 16
        rcopy("p1", r.send_rows.at[c], r.p1.at[z_lo, z_hi], d, z, at_z(c)).start()

    @pl.loop(0, 8)
    def _(i):
        c = 2 * i + p

        @pl.when(c != z)
        def _():
            arrived("wz", r.wb.at[core, c // 8, y, (c % 8) // 2, j], c, at_z(c))

    def w_a(v):
        return r.wb.at[core, 0, y, :, j_of(v)]

    def w_b(v):
        return r.wb.at[core, 1, v, :, j]

    for d in range(1, 4):
        go("wa1", w_a(x), w_a(x), d, x, at_x((x + d) % 4))
        go("wb1", w_b(y), w_b(y), d, y, at_y((y + d) % 4))
    for d in range(1, 4):
        v = (x + d) % 4
        arrived("wa1", w_a(v), v, at_x(v))
    for d in range(1, 4):
        go("wa2", r.wb.at[core, 0, y], r.wb.at[core, 0, y], d, y, at_y((y + d) % 4))
    for d in range(1, 4):
        v = (y + d) % 4
        arrived("wb1", w_b(v), v, at_y(v))
    b_mine = r.wb.at[core, 1, :, :, j]
    for d in range(1, 4):
        go("wb2", b_mine, b_mine, d, x, at_x((x + d) % 4))
    go("wca", r.wb.at[core, 0, y], r.wb.at[core, 0, y], 0, y, pair)
    go("wcb", b_mine, b_mine, 0, x, pair)
    for d in (1, 3, 2):
        v = (y + d) % 4
        arrived("wa2", r.wb.at[core, 0, v], v, at_y(v))
        go("wca", r.wb.at[core, 0, v], r.wb.at[core, 0, v], d, v, pair)
        v = (x + d) % 4
        theirs = r.wb.at[core, 1, :, :, j_of(v)]
        arrived("wb2", theirs, v, at_x(v))
        go("wcb", theirs, theirs, d, v, pair)

    @pl.loop(1, 16)
    def _(d):
        c = (z + d) % 16
        arrived("p1", r.p1.at[c % 8, c // 8], c, at_z(c))

    for d in range(1, 4):
        v = (y + d) % 4
        go("xl", r.p1.at[pl.ds(2 * v, 2)], r.xb.at[:, y], d, y, at_y(v))
    r.xb[:, y] = r.p1[pl.ds(2 * y, 2)]
    perm_v = one_hot(
        256, 256, lambda i: (i % 8) * 32 + (i // 128) * 16 + ((i // 8) % 2) * 8 + (i // 16) % 8
    )
    r.zv[...] = dot(perm_v, r.p1[...].reshape(256, 768)).astype(BF).reshape(8, 2, 16, 768)
    for d in range(1, 8):
        v = (k + d) % 8
        go("zl", r.zv.at[v], r.zb.at[:, k], d, k, at_k(v))
    r.zb[:, k] = r.zv[k]

    for d in range(4):
        v = (y + d) % 4
        arrived("wca", r.wb.at[1 - core, 0, v], v, pair)
        v = (x + d) % 4
        arrived("wcb", r.wb.at[1 - core, 1, :, :, j_of(v)], v, pair)

    gain_row, bias_row = r.gain[...].reshape(1, 768), r.bias[...].reshape(1, 768)
    row_i = lax.broadcasted_iota(jnp.int32, (128, 128), 0)
    col_i = lax.broadcasted_iota(jnp.int32, (128, 128), 1)

    def home(idx, rows, same):
        here = slice(idx * 128, (idx + 1) * 128)
        f = rows.astype(F32)
        t = f[:, :8].reshape(128, 768)
        c16 = f[:, 8:].reshape(128, 768).astype(BF)
        centred = t - jnp.mean(t, axis=-1, keepdims=True)
        inv = lax.rsqrt(jnp.mean(centred * centred, axis=-1, keepdims=True) + EPS)
        nrm = centred * inv
        normed = (nrm * gain_row + bias_row).astype(BF)
        r.lt[0, :, here] = normed.T
        r.lt[1, :, here] = c16.T
        r.gn_acc[...] = jnp.zeros_like(r.gn_acc)

        @pl.loop(0, 2)
        def _(g):
            def w_of(part):
                blocks = [r.wb[part, g, v].reshape(768, 128) for v in range(4)]
                return jnp.concatenate(blocks, axis=1)

            def heads(proj):
                ones = [swap(proj[:, e:e + 128], proj[:, e + 128:e + 256]) for e in (0, 256)]
                return [
                    jnp.concatenate([ones[0][i], ones[1][i]], axis=1).astype(BF) for i in range(2)
                ]

            def blocks_of(a, b):
                pairs = [swap(a[:, e:e + 128], b[:, e:e + 128]) for e in (0, 128)]
                return jnp.concatenate([*pairs[0], *pairs[1]], axis=1).astype(BF)

            q, kk = heads(dot(normed, w_of(0)))
            low = lax.broadcasted_iota(jnp.int32, (128, 512), 1) % 128 < 64
            w_vu = w_of(1)
            vu = jnp.where(low, dot(normed, w_vu), dot(c16, w_vu))
            v, u = heads(vu)
            lane_head = lax.broadcasted_iota(jnp.int32, (128, 256), 1) // 64

            def spread(a):
                return jnp.concatenate(
                    [jnp.where(lane_head == h, a, jnp.zeros_like(a)) for h in range(4)], axis=0
                )

            qs, ks, vs, us = spread(q), spread(kk), spread(v), spread(u)
            s = dot_nt(q, ks)
            dp = dot_nt(u, vs)
            lows, dss = [], []
            for h in range(4):
                sj = jnp.where(same, s[:, h * 128:(h + 1) * 128] * SCALE, -1e30)
                e = jnp.exp(sj - jnp.max(sj, axis=-1, keepdims=True))
                pr = e / jnp.sum(e, axis=-1, keepdims=True)
                dpj = dp[:, h * 128:(h + 1) * 128]
                delta = jnp.sum(pr * dpj, axis=-1, keepdims=True)
                dss.append((pr * (dpj - delta) * SCALE).astype(BF))
                lows.append(pr.astype(BF))
            p_wide, ds_wide = jnp.concatenate(lows, axis=1), jnp.concatenate(dss, axis=1)
            p_tall, ds_tall = jnp.concatenate(lows, axis=0), jnp.concatenate(dss, axis=0)
            att = dot(p_wide, vs)
            gq = dot(ds_wide, ks)
            gk = dot_tn(ds_tall, qs)
            gv = dot_tn(p_tall, us)
            g_qk = blocks_of(gq, gk)
            r.gs_qk[g, here, :] = g_qk
            r.gs_v[g, here, :] = gv.astype(BF)
            r.gs_a[g, here, :] = att.astype(BF)
            g_v = blocks_of(gv, jnp.zeros_like(gv))
            r.gn_acc[...] += dot_nt(g_qk, w_of(0)) + dot_nt(g_v, w_vu)

        g = r.gn_acc[...]
        part = jnp.concatenate(
            [jnp.sum(g * nrm, axis=0, keepdims=True), jnp.sum(g, axis=0, keepdims=True)], axis=0
        )
        return g, nrm, inv, part

    g, nrm, inv, norm_part = home(0, r.send_rows[...], row_i % 8 == col_i % 8)
    r.gn_y[...] = g
    r.nrm_y[...] = nrm
    r.inv_y[...] = jnp.broadcast_to(inv, (128, 128))

    for d in range(1, 4):
        v = (y + d) % 4
        arrived("xl", r.xb.at[:, v], v, at_y(v))
    half = row_i // 64 == col_i // 64
    g, _, _, part = home(1, r.xb[...].reshape(16, 16, 768), half)
    norm_part = norm_part + part
    r.gx[...] = g.astype(BF).reshape(2, 4, 16, 768)
    for d in range(1, 4):
        v = (y + d) % 4
        go("gx", r.gx.at[:, v], r.xg.at[pl.ds(2 * y, 2)], d, y, at_y(v))
    r.xg[pl.ds(2 * y, 2)] = r.gx[:, y]

    for d in range(1, 8):
        v = (k + d) % 8
        arrived("zl", r.zb.at[:, v], v, at_k(v))
    g, _, _, part = home(2, r.zb[...].reshape(16, 16, 768), half)
    norm_part = norm_part + part
    g4 = g.reshape(2, 8, 8, 768)
    r.gz[...] = jnp.concatenate([g4[0], g4[1]], axis=1).astype(BF)
    for d in range(1, 8):
        v = (k + d) % 8
        go("gz", r.gz.at[v], r.zg.at[k], d, k, at_k(v))
    r.zg[k] = r.gz[k]

    r.nc[core] = norm_part
    go("nc", r.nc.at[core], r.nc.at[core], 0, core, pair)

    def weight_grad(part, g, dest):
        lhs = r.lt[0]
        if part == 0:
            full = dot(lhs, r.gs_qk[g])
            blocks = [full[:, e:e + 128] for e in range(0, 512, 128)]
        else:
            gv, ga = dot(lhs, r.gs_v[g]), dot(r.lt[1], r.gs_a[g])
            blocks = []
            for e in (0, 128):
                blocks.extend(swap(gv[:, e:e + 128], ga[:, e:e + 128]))
        for v in range(4):
            dest[g, v] = blocks[v].astype(dest.dtype)

    for g in range(2):
        for part in range(2):
            @pl.when(core == 1 - part)
            def _():
                weight_grad(part, g, r.gw_send)
        go("c", r.gw_send.at[g], r.gw_recv.at[g], g, g, pair)
    for g in range(2):
        for part in range(2):
            @pl.when(core == part)
            def _():
                weight_grad(part, g, r.gw_own)

    for d in range(1, 4):
        v = (y + d) % 4
        arrived("gx", r.xg.at[pl.ds(2 * v, 2)], v, at_y(v))
    for d in range(1, 8):
        v = (k + d) % 8
        arrived("gz", r.zg.at[v], v, at_k(v))
    perm_g = one_hot(128, 128, lambda i: (i % 16) * 8 + i // 16)
    total = dot(perm_g, r.zg[...].reshape(128, 768)) + r.xg[...].reshape(128, 768).astype(F32)
    total = total.reshape(16, 8, 768)
    total = jnp.concatenate([total[:, :, :384], total[:, :, 384:]], axis=1).astype(BF)
    r.rb[...] = total.reshape(8, 2, 16, 384)

    @pl.loop(1, 16)
    def _(d):
        c = (z + d) % 16
        rcopy("rt", r.rb.at[c % 8, c // 8], r.ret.at[z], d, z, at_z(c)).start()

    r.ret[z] = r.rb[z_lo, z_hi]

    arrived("nc", r.nc.at[1 - core], 1 - core, pair)
    r.ny[y] = r.nc[0] + r.nc[1]
    for d in range(1, 4):
        go("ny", r.ny.at[y], r.ny.at[y], d, y, at_y((y + d) % 4))

    arrived("c", r.gw_recv.at[0], 0, pair)
    for d in (2, 1, 3, 0):
        v = (y + d) % 4
        r.a1s[v] = (r.gw_own[0, v] + r.gw_recv[0, v].astype(F32)).astype(BF)
        if d:
            go("a1", r.a1s.at[v], r.a1r.at[y], d, y, at_y(v))
    r.a1r[y] = r.a1s[y]
    arrived("c", r.gw_recv.at[1], 1, pair)
    both = (r.gw_own[1] + r.gw_recv[1].astype(F32)).astype(BF).reshape(4, 4, 4, 48, 128)
    for e in range(4):
        r.b1s[e] = both[:, :, e]
    for d in (2, 1, 3):
        v = (x + d) % 4
        go("b1", r.b1s.at[j_of(v)], r.b1r.at[x], d, x, at_x(v))
    r.b1r[x] = r.b1s[j]

    for d in range(1, 4):
        v = (y + d) % 4
        arrived("ny", r.ny.at[v], v, at_y(v))
    r.nx[x] = (r.ny[0] + r.ny[1]) + (r.ny[2] + r.ny[3])
    for d in range(1, 4):
        go("nx", r.nx.at[x], r.nx.at[x], d, x, at_x((x + d) % 4))

    def four(ref):
        return (ref[0].astype(F32) + ref[1].astype(F32)) + (ref[2].astype(F32) + ref[3].astype(F32))

    for d in range(1, 4):
        v = (y + d) % 4
        arrived("a1", r.a1r.at[v], v, at_y(v))
    a_sum = four(r.a1r).astype(BF).reshape(4, 4, 48, 128)
    for e in range(4):
        r.a2s[e] = a_sum[:, e]
    for d in (2, 1, 3):
        v = (x + d) % 4
        go("a2", r.a2s.at[j_of(v)], r.a2r.at[x], d, x, at_x(v))
    r.a2r[x] = r.a2s[j]
    for d in range(1, 4):
        v = (x + d) % 4
        arrived("b1", r.b1r.at[v], v, at_x(v))
    r.b2s[...] = four(r.b1r).astype(BF)
    for d in (2, 1, 3):
        v = (y + d) % 4
        go("b2", r.b2s.at[v], r.b2r.at[y], d, y, at_y(v))
    r.b2r[y] = r.b2s[y]

    for d in range(1, 4):
        v = (x + d) % 4
        arrived("nx", r.nx.at[v], v, at_x(v))
    r.nz[z] = (r.nx[0] + r.nx[1]) + (r.nx[2] + r.nx[3])

    @pl.loop(1, 16)
    def _(d):
        c = (z + d) % 16
        rcopy("nz", r.nz.at[z], r.nz.at[z], d, z, at_z(c)).start()

    for d in range(1, 4):
        v = (x + d) % 4
        arrived("a2", r.a2r.at[v], v, at_x(v))
    r.zs[0] = four(r.a2r).astype(BF)
    for d in range(1, 4):
        v = (y + d) % 4
        arrived("b2", r.b2r.at[v], v, at_y(v))
    r.zs[1] = four(r.b2r).astype(BF)

    def z_copy(i):
        c = 2 * i + p
        return rcopy("z", r.zs.at[c // 8, (c % 8) // 2], r.zr.at[z], i, z, at_z(c))

    @pl.loop(0, 8)
    def _(i):
        @pl.when(2 * i + p != z)
        def _():
            z_copy(i).start()

    @pl.when(holder)
    def _():
        r.zr[z] = r.zs[z_hi, z_lo // 2]

    @pl.loop(1, 16)
    def _(d):
        c = (z + d) % 16
        arrived("rt", r.ret.at[c], c, at_z(c))

    back = r.ret[...].astype(F32)
    back = jnp.concatenate([back[:, :8], back[:, 8:]], axis=2).reshape(128, 768)
    scaled = (r.gn_y[...] + back) * gain_row
    nrm = r.nrm_y[...]
    m1 = jnp.mean(scaled, axis=-1, keepdims=True)
    m2 = jnp.mean(scaled * nrm, axis=-1, keepdims=True)
    c_rows = r.send_rows[...].astype(F32)[:, 8:].reshape(128, 768)
    rows = (c_rows + r.inv_y[:, :1] * (scaled - m1 - nrm * m2)).astype(BF)
    perm_b = one_hot(128, 128, lambda i: (i % 16) * 8 + i // 16)
    r.tok_out[...] = dot(perm_b, rows).astype(BF)
    store_tok = pltpu.make_async_copy(r.tok_out, tok_res, lsem.at[5])
    store_tok.start()

    @pl.loop(1, 16)
    def _(d):
        c = (z + d) % 16
        arrived("nz", r.nz.at[c], c, at_z(c))

    norm_total = r.nz[0]
    for c in range(1, 16):
        norm_total = norm_total + r.nz[c]
    r.norm_out[...] = norm_total
    store_norm = pltpu.make_async_copy(r.norm_out, norm_res, lsem.at[6])
    store_norm.start()

    def final_copies():
        return [rcopy("f", r.qr.at[core], r.qr.at[core], d, core, quad(d)[1]) for d in range(1, 4)]

    @pl.when(holder)
    def _():
        @pl.loop(1, 16)
        def _(d):
            c = (z + d) % 16
            arrived("z", r.zr.at[c], c, at_z(c))

        z_total = r.zr[0].astype(F32)
        for c in range(1, 16):
            z_total = z_total + r.zr[c].astype(F32)
        r.qr[core] = z_total
        for copy in final_copies():
            copy.start()
        arrived("f", r.qr.at[1 - core], 1 - core, pair)

    @pl.when(jnp.logical_not(holder))
    def _():
        for d in range(2):
            arrived("f", r.qr.at[d], d, at_k((x + 1 - 2 * p) * 2 + d))

    store_w = pltpu.make_async_copy(r.qr, w_res, lsem.at[7])
    store_w.start()

    for copy in sends:
        copy.wait_send()

    @pl.loop(1, 16)
    def _(d):
        c = (z + d) % 16
        dev = at_z(c)
        rcopy("p1", r.send_rows.at[c], r.p1.at[z_lo, z_hi], d, z, dev).wait_send()
        rcopy("rt", r.rb.at[c % 8, c // 8], r.ret.at[z], d, z, dev).wait_send()
        rcopy("nz", r.nz.at[z], r.nz.at[z], d, z, dev).wait_send()

    @pl.loop(0, 8)
    def _(i):
        @pl.when(2 * i + p != z)
        def _():
            z_copy(i).wait_send()

    @pl.when(holder)
    def _():
        @pl.loop(1, 16)
        def _(d):
            rcopy("wz", r.wpart.at[core], w_mine, d, z, at_z((z + d) % 16)).wait_send()

        for copy in final_copies():
            copy.wait_send()

    store_tok.wait()
    store_norm.wait()
    store_w.wait()


def per_device(tokens, cotangent, weights, norm_gain, norm_bias):
    scratch = list(BUFFERS.values())
    for count in SEMAPHORES.values():
        scratch += [pltpu.SemaphoreType.DMA((count,))] * 2
    scratch.append(pltpu.SemaphoreType.DMA((8,)))
    anywhere = pl.BlockSpec(memory_space=pl.ANY)
    grad_tok, grad_w, grad_norm = pl.pallas_call(
        kernel,
        out_shape=(
            jax.ShapeDtypeStruct((128, 768), BF),
            jax.ShapeDtypeStruct((2, 48, 128), F32),
            jax.ShapeDtypeStruct((2, 768), F32),
        ),
        in_specs=[anywhere] * 5,
        out_specs=(anywhere,) * 3,
        scratch_shapes=scratch,
        compiler_params=pltpu.CompilerParams(
            collective_id=0, has_side_effects=True, vmem_limit_bytes=52 * 1024 * 1024
        ),
        name="axial_backward",
    )(tokens.reshape(128, 768), cotangent.reshape(128, 768), weights, norm_gain, norm_bias)
    member = lax.axis_index("slab") % 4
    mine = lax.dynamic_slice(grad_w, (0, member * 12, 0), (2, 12, 128))
    mine = mine.reshape(2, 12, 2, 64).transpose(1, 0, 2, 3).reshape(12, 4, 64)
    return grad_tok.reshape(tokens.shape), mine, grad_norm


def solution(mesh):
    return jax.shard_map(
        per_device,
        mesh=mesh,
        in_specs=(
            P("slab", "head", None, None),
            P("slab", "head", None, None),
            P("slab", None, "head"),
            P(),
            P(),
        ),
        out_specs=(P("slab", "head", None, None), P("slab", None, "head"), P()),
        check_vma=False,
    )
```

```python
import types

import jax
import jax.numpy as jnp
from jax import lax
from jax.experimental import pallas as pl
from jax.experimental.pallas import tpu as pltpu
from jax.sharding import PartitionSpec as P

MESH = pl.DeviceIdType.MESH
BF = jnp.bfloat16
F32 = jnp.float32
EPS = 1e-05
SCALE = 0.125
VM = pltpu.VMEM

BUFFERS = {
    "tok": VM((128, 768), BF),
    "cot": VM((128, 768), BF),
    "wraw": VM((12, 4, 64), BF),
    "gain": VM((768,), F32),
    "bias": VM((768,), F32),
    "wq": VM((4, 16, 256), BF),
    "wpart": VM((2, 48, 128), BF),
    "wb": VM((2, 2, 4, 4, 4, 48, 128), BF),
    "wsep": VM((4, 2, 768, 256), BF),
    "send_rows": VM((2, 16, 16, 384), BF),
    "p1": VM((2, 8, 2, 16, 384), BF),
    "xb": VM((2, 2, 4, 2, 16, 384), BF),
    "zv": VM((2, 8, 2, 16, 384), BF),
    "zb": VM((2, 2, 8, 16, 384), BF),
    "lt": VM((2, 768, 384), BF),
    "normed": VM((3, 128, 768), BF),
    "c16": VM((3, 128, 768), BF),
    "nrm": VM((3, 128, 768), F32),
    "gn": VM((3, 128, 768), F32),
    "gs_qk": VM((2, 384, 512), BF),
    "gs_v": VM((2, 384, 256), BF),
    "gs_a": VM((2, 384, 256), BF),
    "inv_y": VM((128, 128), F32),
    "gx": VM((2, 4, 16, 768), BF),
    "xg": VM((8, 16, 768), BF),
    "gz": VM((8, 16, 768), BF),
    "zg": VM((8, 16, 768), BF),
    "rb": VM((8, 2, 16, 384), BF),
    "ret": VM((16, 16, 384), BF),
    "gw_send": VM((2, 4, 768, 128), BF),
    "gw_recv": VM((2, 4, 768, 128), BF),
    "gw_own": VM((2, 4, 768, 128), F32),
    "a1s": VM((2, 4, 2, 4, 48, 128), BF),
    "a1r": VM((2, 4, 2, 4, 48, 128), BF),
    "b1s": VM((2, 4, 4, 2, 48, 128), BF),
    "b1r": VM((2, 4, 4, 2, 48, 128), BF),
    "a2s": VM((2, 4, 2, 48, 128), BF),
    "a2r": VM((2, 4, 2, 48, 128), BF),
    "b2s": VM((2, 4, 2, 48, 128), BF),
    "b2r": VM((2, 4, 2, 48, 128), BF),
    "zs": VM((2, 4, 48, 128), BF),
    "zr": VM((16, 48, 128), BF),
    "qr": VM((2, 48, 128), F32),
    "tok_out": VM((128, 768), BF),
    "norm_out": VM((2, 1, 768), F32),
    "nk": VM((8, 2, 768), F32),
    "ny": VM((4, 1, 768), F32),
    "nz": VM((16, 1, 768), F32),
}
SEMAPHORES = {
    "q": 4, "wz": 16, "wa1": 4, "wb1": 4, "wa2": 4, "wb2": 4, "wca": 4, "wcb": 4,
    "p1": 32, "xl": 8, "zl": 16, "gx": 4, "gz": 8, "rt": 16,
    "c": 2, "a1": 8, "b1": 8, "a2": 8, "b2": 8, "z": 16, "f": 4,
    "nk": 8, "ny": 4, "nz": 16, "no": 2,
}


def one_hot(rows, cols, source):
    dest = lax.broadcasted_iota(jnp.int32, (rows, cols), 0)
    src = lax.broadcasted_iota(jnp.int32, (rows, cols), 1)
    return (source(dest) == src).astype(BF)


def dot(a, b):
    return jnp.dot(a, b, preferred_element_type=F32)


def dot_nt(a, b):
    return lax.dot_general(a, b, (((1,), (1,)), ((), ())), preferred_element_type=F32)


def dot_tn(a, b):
    return lax.dot_general(a, b, (((0,), (0,)), ((), ())), preferred_element_type=F32)


def fold(a):
    return jnp.concatenate([a[:, :, :384], a[:, :, 384:]], axis=1)


def unfold(a):
    a = a.astype(F32)
    return jnp.concatenate([a[:, :8], a[:, 8:]], axis=2).reshape(-1, 768)


def swap(a, b):
    low = lax.broadcasted_iota(jnp.int32, a.shape, 1) < 64
    return jnp.where(low, a, pltpu.roll(b, 64, 1)), jnp.where(low, pltpu.roll(a, 64, 1), b)


def kernel(tok_in, cot_in, w_in, gain_in, bias_in, tok_res, w_res, norm_res, *refs):
    names = list(BUFFERS)
    r = types.SimpleNamespace(**dict(zip(names, refs)))
    rest = refs[len(names):]
    ssem = {n: rest[2 * i] for i, n in enumerate(SEMAPHORES)}
    rsem = {n: rest[2 * i + 1] for i, n in enumerate(SEMAPHORES)}
    lsem = rest[-1]

    slab = lax.axis_index("slab")
    head = lax.axis_index("head")
    z_lo, x, core = slab // 8, (slab // 2) % 4, slab % 2
    y, z_hi = head // 2, head % 2
    z = z_hi * 8 + z_lo
    k = x * 2 + core
    p = x % 2
    j = 2 * p + x // 2
    member = p * 2 + core
    holder = z_lo % 2 == p

    def at_z(c):
        return ((c % 8) * 8 + k, y * 2 + c // 8)

    def at_y(v):
        return (slab, v * 2 + z_hi)

    def at_k(v):
        return (z_lo * 8 + v, head)

    def at_x(v):
        return at_k(v * 2 + core)

    def j_of(v):
        return 2 * (v % 2) + v // 2

    pair = at_k(x * 2 + 1 - core)

    def rcopy(name, src, dst, si, ri, dev):
        return pltpu.make_async_remote_copy(
            src_ref=src, dst_ref=dst, send_sem=ssem[name].at[si], recv_sem=rsem[name].at[ri],
            device_id=dev, device_id_type=MESH,
        )

    sends = []

    def go(*args):
        copy = rcopy(*args)
        copy.start()
        sends.append(copy)

    def arrived(name, dst, ri, dev):
        rcopy(name, dst, dst, 0, ri, dev).wait_recv()

    loads = [
        pltpu.make_async_copy(src, dst, lsem.at[i])
        for i, (src, dst) in enumerate(
            ((w_in, r.wraw), (tok_in, r.tok), (cot_in, r.cot), (gain_in, r.gain), (bias_in, r.bias))
        )
    ]
    for load in loads:
        load.start()

    barrier = pltpu.get_barrier_semaphore()

    @pl.loop(1, 16)
    def _(d):
        pl.semaphore_signal(barrier, inc=1, device_id=at_z((z + d) % 16), device_id_type=MESH)

    for d in range(1, 4):
        pl.semaphore_signal(barrier, inc=1, device_id=at_y((y + d) % 4), device_id_type=MESH)
    for d in range(1, 8):
        pl.semaphore_signal(barrier, inc=1, device_id=at_k((k + d) % 8), device_id_type=MESH)

    loads[0].wait()
    wide = jnp.concatenate([r.wraw[:, c, :].astype(F32) for c in range(4)], axis=1)
    wide = jnp.concatenate([wide, jnp.zeros((4, 256), F32)], axis=0)
    r.wq[member] = wide.astype(BF)
    pl.semaphore_wait(barrier, 25)

    def quad(d):
        other = (member + d) % 4
        return other, at_k(((other // 2) + 2 * (x // 2)) * 2 + other % 2)

    for d in range(1, 4):
        other, dev = quad(d)
        go("q", r.wq.at[member], r.wq.at[member], d, member, dev)

    for load in loads[1:]:
        load.wait()

    perm = one_hot(128, 128, lambda i: (i % 8) * 16 + i // 8)
    for e, ref in enumerate((r.tok, r.cot)):
        r.send_rows[e] = fold(dot(perm, ref[...]).reshape(16, 8, 768)).astype(BF)

    def token_copy(e, d):
        c = (z + d) % 16
        return rcopy("p1", r.send_rows.at[e, c], r.p1.at[e, z_lo, z_hi], 16 * e + d, 16 * e + z, at_z(c))

    def token_sends(e, start, stop):
        @pl.loop(start, stop)
        def _(i):
            token_copy(e, 8 + (1 - 2 * (i % 2)) * ((i + 1) // 2)).start()

    gain_row, bias_row = r.gain[...].reshape(1, 768), r.bias[...].reshape(1, 768)

    def prepare_cotangent(idx, rows):
        c16 = unfold(rows).astype(BF)
        r.lt[1, :, idx * 128:(idx + 1) * 128] = c16.T
        r.c16[idx] = c16

    def prepare(idx, rows):
        here = slice(idx * 128, (idx + 1) * 128)
        t = unfold(rows)
        centred = t - jnp.mean(t, axis=-1, keepdims=True)
        inv = lax.rsqrt(jnp.mean(centred * centred, axis=-1, keepdims=True) + EPS)
        nrm = centred * inv
        normed = (nrm * gain_row + bias_row).astype(BF)
        r.lt[0, :, here] = normed.T
        r.normed[idx] = normed
        r.nrm[idx] = nrm
        r.gn[idx] = jnp.zeros((128, 768), F32)
        return inv

    for d in range(1, 4):
        other, dev = quad(d)
        arrived("q", r.wq.at[other], other, dev)
    stack = one_hot(48, 64, lambda i: (i // 12) * 16 + i % 12)
    block = dot(stack, r.wq[...].reshape(64, 256)).astype(BF)
    r.wpart[0] = block[:, :128]
    r.wpart[1] = block[:, 128:]

    w_mine = r.wb.at[core, z_hi, y, z_lo // 2, j]

    @pl.when(holder)
    def _():
        w_mine[...] = r.wpart[core]

        @pl.loop(1, 16)
        def _(d):
            rcopy("wz", r.wpart.at[core], w_mine, d, z, at_z((z + d) % 16)).start()

    r.inv_y[...] = jnp.broadcast_to(prepare(0, r.send_rows[0]), (128, 128))
    prepare_cotangent(0, r.send_rows[1])

    @pl.loop(0, 8)
    def _(i):
        c = 2 * i + p

        @pl.when(c != z)
        def _():
            arrived("wz", r.wb.at[core, c // 8, y, (c % 8) // 2, j], c, at_z(c))

    def w_a(v):
        return r.wb.at[core, 0, y, :, j_of(v)]

    def w_b(v):
        return r.wb.at[core, 1, v, :, j]

    for d in range(1, 4):
        go("wa1", w_a(x), w_a(x), d, x, at_x((x + d) % 4))
        go("wb1", w_b(y), w_b(y), d, y, at_y((y + d) % 4))
    token_sends(0, 0, 8)
    for e in range(2):
        r.p1[e, z_lo, z_hi] = r.send_rows[e, z]

    for d in range(1, 4):
        v = (x + d) % 4
        arrived("wa1", w_a(v), v, at_x(v))
    a_mine, b_mine = r.wb.at[core, 0, y], r.wb.at[core, 1, :, :, j]
    go("wca", a_mine, a_mine, 0, y, pair)
    for d, span in ((1, (8, 10)), (3, (10, 12)), (2, (12, 15))):
        go("wa2", a_mine, a_mine, d, y, at_y((y + d) % 4))
        token_sends(0, *span)
    for d in range(1, 4):
        v = (y + d) % 4
        arrived("wb1", w_b(v), v, at_y(v))
    go("wcb", b_mine, b_mine, 0, x, pair)
    for d, span in ((1, (0, 4)), (3, (4, 8)), (2, (8, 15))):
        go("wb2", b_mine, b_mine, d, x, at_x((x + d) % 4))
        token_sends(1, *span)

    perm_v = one_hot(
        256, 256, lambda i: (i % 8) * 32 + (i // 128) * 16 + ((i // 8) % 2) * 8 + (i // 16) % 8
    )

    def second_hop(e):
        @pl.loop(1, 16)
        def _(d):
            c = (z + d) % 16
            arrived("p1", r.p1.at[e, c % 8, c // 8], 16 * e + c, at_z(c))

        for d in range(1, 4):
            v = (y + d) % 4
            go("xl", r.p1.at[e, pl.ds(2 * v, 2)], r.xb.at[e, :, y], 4 * e + d, 4 * e + y, at_y(v))
        r.xb[e, :, y] = r.p1[e, pl.ds(2 * y, 2)]
        r.zv[e] = dot(perm_v, r.p1[e].reshape(256, 384)).astype(BF).reshape(8, 2, 16, 384)
        for d in range(1, 8):
            v = (k + d) % 8
            go("zl", r.zv.at[e, v], r.zb.at[e, :, k], 8 * e + d, 8 * e + k, at_k(v))
        r.zb[e, :, k] = r.zv[e, k]

    def lines_arrived(e):
        for d in range(1, 4):
            v = (y + d) % 4
            arrived("xl", r.xb.at[e, :, v], 4 * e + v, at_y(v))
        for d in range(1, 8):
            v = (k + d) % 8
            arrived("zl", r.zb.at[e, :, v], 8 * e + v, at_k(v))

    second_hop(0)

    for d in (1, 3, 2):
        v = (y + d) % 4
        theirs = r.wb.at[core, 0, v]
        arrived("wa2", theirs, v, at_y(v))
        go("wca", theirs, theirs, d, v, pair)
        v = (x + d) % 4
        theirs = r.wb.at[core, 1, :, :, j_of(v)]
        arrived("wb2", theirs, v, at_x(v))
        go("wcb", theirs, theirs, d, v, pair)
    second_hop(1)

    for d in range(4):
        v = (y + d) % 4
        arrived("wca", r.wb.at[1 - core, 0, v], v, pair)
        v = (x + d) % 4
        arrived("wcb", r.wb.at[1 - core, 1, :, :, j_of(v)], v, pair)

    row_i = lax.broadcasted_iota(jnp.int32, (128, 128), 0)
    col_i = lax.broadcasted_iota(jnp.int32, (128, 128), 1)

    @pl.loop(0, 4)
    def _(i):
        part, g = i // 2, i % 2
        for e in range(2):
            both = [r.wb[part, g, 2 * e + h].reshape(768, 128).astype(F32) for h in range(2)]
            for h, block in enumerate(swap(*both)):
                r.wsep[2 * part + h, g, :, e * 128:(e + 1) * 128] = block.astype(BF)

    def lines(q, kk, v, u, same):
        lane_head = lax.broadcasted_iota(jnp.int32, (128, 256), 1) // 64

        def spread(a):
            return jnp.concatenate(
                [jnp.where(lane_head == h, a, jnp.zeros_like(a)) for h in range(4)], axis=0
            )

        qs, ks, vs, us = spread(q), spread(kk), spread(v), spread(u)
        s = dot_nt(q, ks)
        dp = dot_nt(u, vs)
        lows, dss = [], []
        for h in range(4):
            sj = jnp.where(same, s[:, h * 128:(h + 1) * 128] * SCALE, -1e30)
            e = jnp.exp(sj - jnp.max(sj, axis=-1, keepdims=True))
            pr = e / jnp.sum(e, axis=-1, keepdims=True)
            dpj = dp[:, h * 128:(h + 1) * 128]
            delta = jnp.sum(pr * dpj, axis=-1, keepdims=True)
            dss.append((pr * (dpj - delta) * SCALE).astype(BF))
            lows.append(pr.astype(BF))
        p_wide, ds_wide = jnp.concatenate(lows, axis=1), jnp.concatenate(dss, axis=1)
        p_tall, ds_tall = jnp.concatenate(lows, axis=0), jnp.concatenate(dss, axis=0)
        return dot(ds_wide, ks), dot_tn(ds_tall, qs), dot_tn(p_tall, us), dot(p_wide, vs)

    def blocks_of(a, b):
        pairs = [swap(a[:, e:e + 128], b[:, e:e + 128]) for e in (0, 128)]
        return jnp.concatenate([*pairs[0], *pairs[1]], axis=1).astype(BF)

    def home(first, count, g, same):
        normed = r.normed[first:first + count].reshape(count * 128, 768)
        c16 = r.c16[first:first + count].reshape(count * 128, 768)
        feats = [dot(normed, r.wsep[c, g]).astype(BF) for c in range(3)]
        feats.append(dot(c16, r.wsep[3, g]).astype(BF))
        grads = [[], [], []]
        for i in range(count):
            here = slice(i * 128, (i + 1) * 128)
            there = slice((first + i) * 128, (first + i + 1) * 128)
            gq, gk, gv, att = lines(*[a[here] for a in feats], same)
            r.gs_qk[g, there, :] = blocks_of(gq, gk)
            r.gs_v[g, there, :] = gv.astype(BF)
            r.gs_a[g, there, :] = att.astype(BF)
            for c, one in enumerate((gq, gk, gv)):
                grads[c].append(one.astype(BF))
        back = [dot_nt(jnp.concatenate(grads[c], axis=0), r.wsep[c, g]) for c in range(3)]
        back = (back[0] + back[1]) + back[2]
        for i in range(count):
            r.gn[first + i] += back[i * 128:(i + 1) * 128]

    @pl.loop(0, 2)
    def _(g):
        home(0, 1, g, row_i % 8 == col_i % 8)

    half = row_i // 64 == col_i // 64
    lines_arrived(0)
    prepare(1, r.xb[0].reshape(16, 16, 384))
    prepare(2, r.zb[0].reshape(16, 16, 384))
    lines_arrived(1)
    prepare_cotangent(1, r.xb[1].reshape(16, 16, 384))
    prepare_cotangent(2, r.zb[1].reshape(16, 16, 384))

    home(1, 2, 0, half)

    def weight_grad(part, g, dest):
        lhs = r.lt[0]
        if part == 0:
            full = dot(lhs, r.gs_qk[g])
            blocks = [full[:, e:e + 128] for e in range(0, 512, 128)]
        else:
            gv, ga = dot(lhs, r.gs_v[g]), dot(r.lt[1], r.gs_a[g])
            blocks = []
            for e in (0, 128):
                blocks.extend(swap(gv[:, e:e + 128], ga[:, e:e + 128]))
        for v in range(4):
            dest[g, v] = blocks[v].astype(dest.dtype)

    def to_other_core(g):
        for part in range(2):
            @pl.when(core == 1 - part)
            def _():
                weight_grad(part, g, r.gw_send)
        go("c", r.gw_send.at[g], r.gw_recv.at[g], g, g, pair)

    def own_part(g):
        for part in range(2):
            @pl.when(core == part)
            def _():
                weight_grad(part, g, r.gw_own)

    def four(ref):
        return (ref[0].astype(F32) + ref[1].astype(F32)) + (ref[2].astype(F32) + ref[3].astype(F32))

    def sum_first(g, between=lambda i: None):
        arrived("c", r.gw_recv.at[g], g, pair)
        for v in range(4):
            both = (r.gw_own[g, v] + r.gw_recv[g, v].astype(F32)).astype(BF).reshape(4, 4, 48, 128)
            r.a1s[g, v] = both[:2]
            for e in range(4):
                r.b1s[g, e, v] = both[2:, e]
        for i, d in enumerate((2, 1, 3)):
            between(i)
            v = (y + d) % 4
            go("a1", r.a1s.at[g, v], r.a1r.at[g, y], 4 * g + d, 4 * g + y, at_y(v))
            v = (x + d) % 4
            go("b1", r.b1s.at[g, j_of(v)], r.b1r.at[g, x], 4 * g + d, 4 * g + x, at_x(v))
        r.a1r[g, y] = r.a1s[g, y]
        r.b1r[g, x] = r.b1s[g, j]

    def sum_second(g):
        for d in range(1, 4):
            v = (y + d) % 4
            arrived("a1", r.a1r.at[g, v], 4 * g + v, at_y(v))
        a_sum = four(r.a1r.at[g]).astype(BF)
        for e in range(4):
            r.a2s[g, e] = a_sum[:, e]
        for d in (2, 1, 3):
            v = (x + d) % 4
            go("a2", r.a2s.at[g, j_of(v)], r.a2r.at[g, x], 4 * g + d, 4 * g + x, at_x(v))
        r.a2r[g, x] = r.a2s[g, j]
        for d in range(1, 4):
            v = (x + d) % 4
            arrived("b1", r.b1r.at[g, v], 4 * g + v, at_x(v))
        r.b2s[g] = four(r.b1r.at[g]).astype(BF)
        for d in (2, 1, 3):
            v = (y + d) % 4
            go("b2", r.b2s.at[g, v], r.b2r.at[g, y], 4 * g + d, 4 * g + y, at_y(v))
        r.b2r[g, y] = r.b2s[g, y]

    def z_copy(g, i):
        c = 8 * g + 2 * i + p
        return rcopy("z", r.zs.at[g, i], r.zr.at[z], 4 * g + i, z, at_z(c))

    def sum_third(g):
        for d in range(1, 4):
            v = (x + d) % 4
            arrived("a2", r.a2r.at[g, v], 4 * g + v, at_x(v))
        r.zs[g, 0:2] = four(r.a2r.at[g]).astype(BF)
        for d in range(1, 4):
            v = (y + d) % 4
            arrived("b2", r.b2r.at[g, v], 4 * g + v, at_y(v))
        r.zs[g, 2:4] = four(r.b2r.at[g]).astype(BF)

        @pl.loop(0, 4)
        def _(i):
            @pl.when(8 * g + 2 * i + p != z)
            def _():
                z_copy(g, i).start()

    home(1, 2, 1, half)

    g = r.gn[1]
    r.gx[...] = g.astype(BF).reshape(2, 4, 16, 768)
    for d in range(1, 4):
        v = (y + d) % 4
        go("gx", r.gx.at[:, v], r.xg.at[pl.ds(2 * y, 2)], d, y, at_y(v))
    r.xg[pl.ds(2 * y, 2)] = r.gx[:, y]
    g4 = r.gn[2].reshape(2, 8, 8, 768)
    r.gz[...] = jnp.concatenate([g4[0], g4[1]], axis=1).astype(BF)
    for d in range(1, 8):
        v = (k + d) % 8
        go("gz", r.gz.at[v], r.zg.at[k], d, k, at_k(v))
    r.zg[k] = r.gz[k]

    parts = [r.gn[0] * r.nrm[0] + r.gn[1] * r.nrm[1] + r.gn[2] * r.nrm[2], r.gn[0] + r.gn[1] + r.gn[2]]
    r.nk[k] = jnp.concatenate([jnp.sum(e, axis=0, keepdims=True) for e in parts], axis=0)
    for d in range(1, 8):
        go("nk", r.nk.at[k], r.nk.at[k], d, k, at_k((k + d) % 8))

    to_other_core(0)
    to_other_core(1)
    own_part(0)
    sum_first(0)
    own_part(1)

    for d in range(1, 8):
        v = (k + d) % 8
        arrived("nk", r.nk.at[v], v, at_k(v))
    both = r.nk[0]
    for v in range(1, 8):
        both = both + r.nk[v]
    r.ny[y] = jnp.where(core == 0, both[0:1], both[1:2])
    for d in range(1, 4):
        go("ny", r.ny.at[y], r.ny.at[y], d, y, at_y((y + d) % 4))

    for d in range(1, 4):
        v = (y + d) % 4
        arrived("gx", r.xg.at[pl.ds(2 * v, 2)], v, at_y(v))
    for d in range(1, 8):
        v = (k + d) % 8
        arrived("gz", r.zg.at[v], v, at_k(v))
    perm_g = one_hot(128, 128, lambda i: (i % 16) * 8 + i // 16)
    total = dot(perm_g, r.zg[...].reshape(128, 768)) + r.xg[...].reshape(128, 768).astype(F32)
    r.rb[...] = fold(total.reshape(16, 8, 768)).astype(BF).reshape(8, 2, 16, 384)

    def return_sends(i):
        @pl.loop(1 + 5 * i, 6 + 5 * i)
        def _(d):
            c = (z + d) % 16
            rcopy("rt", r.rb.at[c % 8, c // 8], r.ret.at[z], d, z, at_z(c)).start()

    sum_first(1, return_sends)
    for d in range(1, 4):
        v = (y + d) % 4
        arrived("ny", r.ny.at[v], v, at_y(v))
    r.nz[z] = (r.ny[0] + r.ny[1]) + (r.ny[2] + r.ny[3])

    r.ret[z] = r.rb[z_lo, z_hi]

    @pl.loop(1, 16)
    def _(d):
        rcopy("nz", r.nz.at[z], r.nz.at[z], d, z, at_z((z + d) % 16)).start()

    sum_second(0)
    sum_second(1)

    sum_third(0)
    sum_third(1)

    @pl.when(holder)
    def _():
        r.zr[z] = r.zs[z_hi, z_lo // 2]

    @pl.loop(1, 16)
    def _(d):
        c = (z + d) % 16
        arrived("rt", r.ret.at[c], c, at_z(c))

    scaled = (r.gn[0] + unfold(r.ret[...])) * gain_row
    nrm = r.nrm[0]
    m1 = jnp.mean(scaled, axis=-1, keepdims=True)
    m2 = jnp.mean(scaled * nrm, axis=-1, keepdims=True)
    c_rows = r.c16[0].astype(F32)
    rows = (c_rows + r.inv_y[:, :1] * (scaled - m1 - nrm * m2)).astype(BF)
    perm_b = one_hot(128, 128, lambda i: (i % 16) * 8 + i // 16)
    r.tok_out[...] = dot(perm_b, rows).astype(BF)
    store_tok = pltpu.make_async_copy(r.tok_out, tok_res, lsem.at[5])
    store_tok.start()

    @pl.loop(1, 16)
    def _(d):
        c = (z + d) % 16
        arrived("nz", r.nz.at[c], c, at_z(c))

    row = r.nz[0]
    for c in range(1, 16):
        row = row + r.nz[c]
    r.norm_out[core] = row
    go("no", r.norm_out.at[core], r.norm_out.at[core], 0, core, pair)

    def final_copies():
        return [rcopy("f", r.qr.at[core], r.qr.at[core], d, core, quad(d)[1]) for d in range(1, 4)]

    @pl.when(holder)
    def _():
        @pl.loop(1, 16)
        def _(d):
            c = (z + d) % 16
            arrived("z", r.zr.at[c], c, at_z(c))

        z_total = r.zr[0].astype(F32)
        for c in range(1, 16):
            z_total = z_total + r.zr[c].astype(F32)
        r.qr[core] = z_total
        for copy in final_copies():
            copy.start()
        arrived("f", r.qr.at[1 - core], 1 - core, pair)

    @pl.when(jnp.logical_not(holder))
    def _():
        for d in range(2):
            arrived("f", r.qr.at[d], d, at_k((x + 1 - 2 * p) * 2 + d))

    arrived("no", r.norm_out.at[1 - core], 1 - core, pair)
    store_norm = pltpu.make_async_copy(r.norm_out, norm_res, lsem.at[6])
    store_norm.start()
    store_w = pltpu.make_async_copy(r.qr, w_res, lsem.at[7])
    store_w.start()

    for copy in sends:
        copy.wait_send()

    @pl.loop(1, 16)
    def _(d):
        c = (z + d) % 16
        dev = at_z(c)
        for e in range(2):
            token_copy(e, d).wait_send()
        rcopy("rt", r.rb.at[c % 8, c // 8], r.ret.at[z], d, z, dev).wait_send()
        rcopy("nz", r.nz.at[z], r.nz.at[z], d, z, dev).wait_send()

    for g in range(2):
        @pl.loop(0, 4)
        def _(i):
            @pl.when(8 * g + 2 * i + p != z)
            def _():
                z_copy(g, i).wait_send()

    @pl.when(holder)
    def _():
        @pl.loop(1, 16)
        def _(d):
            rcopy("wz", r.wpart.at[core], w_mine, d, z, at_z((z + d) % 16)).wait_send()

        for copy in final_copies():
            copy.wait_send()

    store_tok.wait()
    store_norm.wait()
    store_w.wait()


def per_device(tokens, cotangent, weights, norm_gain, norm_bias):
    scratch = list(BUFFERS.values())
    for count in SEMAPHORES.values():
        scratch += [pltpu.SemaphoreType.DMA((count,))] * 2
    scratch.append(pltpu.SemaphoreType.DMA((8,)))
    anywhere = pl.BlockSpec(memory_space=pltpu.HBM)
    grad_tok, grad_w, grad_norm = pl.pallas_call(
        kernel,
        out_shape=(
            jax.ShapeDtypeStruct((128, 768), BF),
            jax.ShapeDtypeStruct((2, 48, 128), F32),
            jax.ShapeDtypeStruct((2, 1, 768), F32),
        ),
        in_specs=[anywhere] * 5,
        out_specs=(anywhere,) * 3,
        scratch_shapes=scratch,
        compiler_params=pltpu.CompilerParams(
            collective_id=0, has_side_effects=True, vmem_limit_bytes=60 * 1024 * 1024
        ),
        name="axial_backward",
    )(tokens.reshape(128, 768), cotangent.reshape(128, 768), weights, norm_gain, norm_bias)
    member = lax.axis_index("slab") % 4
    mine = lax.dynamic_slice(grad_w, (0, member * 12, 0), (2, 12, 128))
    mine = mine.reshape(2, 12, 2, 64).transpose(1, 0, 2, 3).reshape(12, 4, 64)
    return grad_tok.reshape(tokens.shape), mine, grad_norm.reshape(2, 768)


def solution(mesh):
    return jax.shard_map(
        per_device,
        mesh=mesh,
        in_specs=(
            P("slab", "head", None, None),
            P("slab", "head", None, None),
            P("slab", None, "head"),
            P(),
            P(),
        ),
        out_specs=(P("slab", "head", None, None), P("slab", None, "head"), P()),
        check_vma=False,
    )
```

```python
import types

import jax
import jax.numpy as jnp
from jax import lax
from jax.experimental import pallas as pl
from jax.experimental.pallas import tpu as pltpu
from jax.sharding import PartitionSpec as P

MESH = pl.DeviceIdType.MESH
BF = jnp.bfloat16
F32 = jnp.float32
EPS = 1e-05
SCALE = 0.125
VM = pltpu.VMEM

BUFFERS = {
    "tok": VM((128, 768), BF),
    "cot": VM((128, 768), BF),
    "wraw": VM((12, 4, 64), BF),
    "gain": VM((768,), F32),
    "bias": VM((768,), F32),
    "wq": VM((4, 16, 256), BF),
    "wpart": VM((2, 48, 128), BF),
    "wb": VM((2, 2, 4, 4, 4, 48, 128), BF),
    "wsep": VM((4, 2, 768, 256), BF),
    "send_rows": VM((2, 16, 16, 384), BF),
    "p1": VM((2, 8, 2, 16, 384), BF),
    "xb": VM((2, 2, 4, 2, 16, 384), BF),
    "zv": VM((2, 8, 2, 16, 384), BF),
    "zb": VM((2, 2, 8, 16, 384), BF),
    "lt": VM((2, 768, 384), BF),
    "normed": VM((3, 128, 768), BF),
    "c16": VM((3, 128, 768), BF),
    "nrm": VM((3, 128, 768), F32),
    "gn": VM((3, 128, 768), F32),
    "gs_qk": VM((2, 384, 512), BF),
    "gs_v": VM((2, 384, 256), BF),
    "gs_a": VM((2, 384, 256), BF),
    "inv_y": VM((128, 128), F32),
    "gx": VM((2, 4, 16, 768), BF),
    "xg": VM((8, 16, 768), BF),
    "gz": VM((8, 16, 768), BF),
    "zg": VM((8, 16, 768), BF),
    "rb": VM((8, 2, 16, 384), BF),
    "ret": VM((16, 16, 384), BF),
    "gw_send": VM((2, 4, 768, 128), BF),
    "gw_recv": VM((2, 4, 768, 128), BF),
    "gw_own": VM((2, 4, 768, 128), F32),
    "a1s": VM((2, 4, 2, 4, 48, 128), BF),
    "a1r": VM((2, 4, 2, 4, 48, 128), BF),
    "b1s": VM((2, 4, 4, 2, 48, 128), BF),
    "b1r": VM((2, 4, 4, 2, 48, 128), BF),
    "a2s": VM((2, 4, 2, 48, 128), BF),
    "a2r": VM((2, 4, 2, 48, 128), BF),
    "b2s": VM((2, 4, 2, 48, 128), BF),
    "b2r": VM((2, 4, 2, 48, 128), BF),
    "zs": VM((2, 4, 48, 128), BF),
    "zr": VM((16, 48, 128), BF),
    "qr": VM((2, 48, 128), F32),
    "tok_out": VM((128, 768), BF),
    "norm_out": VM((2, 1, 768), F32),
    "nk": VM((8, 2, 768), F32),
    "ny": VM((4, 1, 768), F32),
    "nz": VM((16, 1, 768), F32),
}
SEMAPHORES = {
    "q": 4, "wz": 16, "wa1": 4, "wb1": 4, "wa2": 4, "wb2": 4, "wca": 4, "wcb": 4,
    "p1": 32, "xl": 8, "zl": 16, "gx": 4, "gz": 8, "rt": 16,
    "c": 2, "a1": 8, "b1": 8, "a2": 8, "b2": 8, "z": 16, "f": 4,
    "nk": 8, "ny": 4, "nz": 16, "no": 2,
}


def one_hot(rows, cols, source):
    dest = lax.broadcasted_iota(jnp.int32, (rows, cols), 0)
    src = lax.broadcasted_iota(jnp.int32, (rows, cols), 1)
    return (source(dest) == src).astype(BF)


def dot(a, b):
    return jnp.dot(a, b, preferred_element_type=F32)


def dot_nt(a, b):
    return lax.dot_general(a, b, (((1,), (1,)), ((), ())), preferred_element_type=F32)


def dot_tn(a, b):
    return lax.dot_general(a, b, (((0,), (0,)), ((), ())), preferred_element_type=F32)


def fold(a):
    return jnp.concatenate([a[:, :, :384], a[:, :, 384:]], axis=1)


def unfold(a):
    a = a.astype(F32)
    return jnp.concatenate([a[:, :8], a[:, 8:]], axis=2).reshape(-1, 768)


def swap(a, b):
    low = lax.broadcasted_iota(jnp.int32, a.shape, 1) < 64
    return jnp.where(low, a, pltpu.roll(b, 64, 1)), jnp.where(low, pltpu.roll(a, 64, 1), b)


def kernel(tok_in, cot_in, w_in, gain_in, bias_in, tok_res, w_res, norm_res, *refs):
    names = list(BUFFERS)
    r = types.SimpleNamespace(**dict(zip(names, refs)))
    rest = refs[len(names):]
    ssem = {n: rest[2 * i] for i, n in enumerate(SEMAPHORES)}
    rsem = {n: rest[2 * i + 1] for i, n in enumerate(SEMAPHORES)}
    lsem = rest[-1]

    slab = lax.axis_index("slab")
    head = lax.axis_index("head")
    z_lo, x, core = slab // 8, (slab // 2) % 4, slab % 2
    y, z_hi = head // 2, head % 2
    z = z_hi * 8 + z_lo
    k = x * 2 + core
    p = x % 2
    j = 2 * p + x // 2
    member = p * 2 + core
    holder = z_lo % 2 == p

    def at_z(c):
        return ((c % 8) * 8 + k, y * 2 + c // 8)

    def at_y(v):
        return (slab, v * 2 + z_hi)

    def at_k(v):
        return (z_lo * 8 + v, head)

    def at_x(v):
        return at_k(v * 2 + core)

    def j_of(v):
        return 2 * (v % 2) + v // 2

    pair = at_k(x * 2 + 1 - core)

    def rcopy(name, src, dst, si, ri, dev):
        return pltpu.make_async_remote_copy(
            src_ref=src, dst_ref=dst, send_sem=ssem[name].at[si], recv_sem=rsem[name].at[ri],
            device_id=dev, device_id_type=MESH,
        )

    sends = []

    def go(*args):
        copy = rcopy(*args)
        copy.start()
        sends.append(copy)

    def arrived(name, dst, ri, dev):
        rcopy(name, dst, dst, 0, ri, dev).wait_recv()

    loads = [
        pltpu.make_async_copy(src, dst, lsem.at[i])
        for i, (src, dst) in enumerate(
            ((w_in, r.wraw), (tok_in, r.tok), (cot_in, r.cot), (gain_in, r.gain), (bias_in, r.bias))
        )
    ]
    for load in loads:
        load.start()

    barrier = pltpu.get_barrier_semaphore()

    @pl.loop(1, 16)
    def _(d):
        pl.semaphore_signal(barrier, inc=1, device_id=at_z((z + d) % 16), device_id_type=MESH)

    for d in range(1, 4):
        pl.semaphore_signal(barrier, inc=1, device_id=at_y((y + d) % 4), device_id_type=MESH)
    for d in range(1, 8):
        pl.semaphore_signal(barrier, inc=1, device_id=at_k((k + d) % 8), device_id_type=MESH)

    loads[0].wait()
    wide = jnp.concatenate([r.wraw[:, c, :].astype(F32) for c in range(4)], axis=1)
    wide = jnp.concatenate([wide, jnp.zeros((4, 256), F32)], axis=0)
    r.wq[member] = wide.astype(BF)
    pl.semaphore_wait(barrier, 25)

    def quad(d):
        other = (member + d) % 4
        return other, at_k(((other // 2) + 2 * (x // 2)) * 2 + other % 2)

    for d in range(1, 4):
        other, dev = quad(d)
        go("q", r.wq.at[member], r.wq.at[member], d, member, dev)

    for load in loads[1:]:
        load.wait()

    perm = one_hot(128, 128, lambda i: (i % 8) * 16 + i // 8)
    for e, ref in enumerate((r.tok, r.cot)):
        r.send_rows[e] = fold(dot(perm, ref[...]).reshape(16, 8, 768)).astype(BF)

    def token_copy(e, d):
        c = (z + d) % 16
        return rcopy("p1", r.send_rows.at[e, c], r.p1.at[e, z_lo, z_hi], 16 * e + d, 16 * e + z, at_z(c))

    def token_sends(e, start, stop):
        @pl.loop(start, stop)
        def _(i):
            token_copy(e, 8 + (1 - 2 * (i % 2)) * ((i + 1) // 2)).start()

    token_sends(0, 0, 3)

    gain_row, bias_row = r.gain[...].reshape(1, 768), r.bias[...].reshape(1, 768)

    def prepare_cotangent(idx, rows):
        c16 = unfold(rows).astype(BF)
        r.lt[1, :, idx * 128:(idx + 1) * 128] = c16.T
        r.c16[idx] = c16

    def prepare(idx, rows):
        here = slice(idx * 128, (idx + 1) * 128)
        t = unfold(rows)
        centred = t - jnp.mean(t, axis=-1, keepdims=True)
        inv = lax.rsqrt(jnp.mean(centred * centred, axis=-1, keepdims=True) + EPS)
        nrm = centred * inv
        normed = (nrm * gain_row + bias_row).astype(BF)
        r.lt[0, :, here] = normed.T
        r.normed[idx] = normed
        r.nrm[idx] = nrm
        r.gn[idx] = jnp.zeros((128, 768), F32)
        return inv

    for d in range(1, 4):
        other, dev = quad(d)
        arrived("q", r.wq.at[other], other, dev)
    stack = one_hot(48, 64, lambda i: (i // 12) * 16 + i % 12)
    block = dot(stack, r.wq[...].reshape(64, 256)).astype(BF)
    r.wpart[0] = block[:, :128]
    r.wpart[1] = block[:, 128:]

    w_mine = r.wb.at[core, z_hi, y, z_lo // 2, j]

    @pl.when(holder)
    def _():
        w_mine[...] = r.wpart[core]

        @pl.loop(1, 16)
        def _(d):
            rcopy("wz", r.wpart.at[core], w_mine, d, z, at_z((z + d) % 16)).start()

    r.inv_y[...] = jnp.broadcast_to(prepare(0, r.send_rows[0]), (128, 128))
    prepare_cotangent(0, r.send_rows[1])

    @pl.loop(0, 8)
    def _(i):
        c = 2 * i + p

        @pl.when(c != z)
        def _():
            arrived("wz", r.wb.at[core, c // 8, y, (c % 8) // 2, j], c, at_z(c))

    def w_a(v):
        return r.wb.at[core, 0, y, :, j_of(v)]

    def w_b(v):
        return r.wb.at[core, 1, v, :, j]

    for d in range(1, 4):
        go("wa1", w_a(x), w_a(x), d, x, at_x((x + d) % 4))
        go("wb1", w_b(y), w_b(y), d, y, at_y((y + d) % 4))
    token_sends(0, 3, 8)
    for e in range(2):
        r.p1[e, z_lo, z_hi] = r.send_rows[e, z]

    for d in range(1, 4):
        v = (x + d) % 4
        arrived("wa1", w_a(v), v, at_x(v))
    a_mine, b_mine = r.wb.at[core, 0, y], r.wb.at[core, 1, :, :, j]
    go("wca", a_mine, a_mine, 0, y, pair)
    for d, span in ((1, (8, 10)), (3, (10, 12)), (2, (12, 15))):
        go("wa2", a_mine, a_mine, d, y, at_y((y + d) % 4))
        token_sends(0, *span)
    for d in range(1, 4):
        v = (y + d) % 4
        arrived("wb1", w_b(v), v, at_y(v))
    go("wcb", b_mine, b_mine, 0, x, pair)
    for d, span in ((1, (0, 4)), (3, (4, 8)), (2, (8, 15))):
        go("wb2", b_mine, b_mine, d, x, at_x((x + d) % 4))
        token_sends(1, *span)

    perm_v = one_hot(
        256, 256, lambda i: (i % 8) * 32 + (i // 128) * 16 + ((i // 8) % 2) * 8 + (i // 16) % 8
    )

    def second_hop(e):
        @pl.loop(1, 16)
        def _(d):
            c = (z + d) % 16
            arrived("p1", r.p1.at[e, c % 8, c // 8], 16 * e + c, at_z(c))

        for d in range(1, 4):
            v = (y + d) % 4
            go("xl", r.p1.at[e, pl.ds(2 * v, 2)], r.xb.at[e, :, y], 4 * e + d, 4 * e + y, at_y(v))
        r.xb[e, :, y] = r.p1[e, pl.ds(2 * y, 2)]
        r.zv[e] = dot(perm_v, r.p1[e].reshape(256, 384)).astype(BF).reshape(8, 2, 16, 384)
        for d in range(1, 8):
            v = (k + d) % 8
            go("zl", r.zv.at[e, v], r.zb.at[e, :, k], 8 * e + d, 8 * e + k, at_k(v))
        r.zb[e, :, k] = r.zv[e, k]

    def lines_arrived(e):
        for d in range(1, 4):
            v = (y + d) % 4
            arrived("xl", r.xb.at[e, :, v], 4 * e + v, at_y(v))
        for d in range(1, 8):
            v = (k + d) % 8
            arrived("zl", r.zb.at[e, :, v], 8 * e + v, at_k(v))

    second_hop(0)

    for d in (1, 3, 2):
        v = (y + d) % 4
        theirs = r.wb.at[core, 0, v]
        arrived("wa2", theirs, v, at_y(v))
        go("wca", theirs, theirs, d, v, pair)
        v = (x + d) % 4
        theirs = r.wb.at[core, 1, :, :, j_of(v)]
        arrived("wb2", theirs, v, at_x(v))
        go("wcb", theirs, theirs, d, v, pair)
    second_hop(1)

    for d in range(4):
        v = (y + d) % 4
        arrived("wca", r.wb.at[1 - core, 0, v], v, pair)
        v = (x + d) % 4
        arrived("wcb", r.wb.at[1 - core, 1, :, :, j_of(v)], v, pair)

    row_i = lax.broadcasted_iota(jnp.int32, (128, 128), 0)
    col_i = lax.broadcasted_iota(jnp.int32, (128, 128), 1)

    @pl.loop(0, 4)
    def _(i):
        part, g = i // 2, i % 2
        for e in range(2):
            both = [r.wb[part, g, 2 * e + h].reshape(768, 128).astype(F32) for h in range(2)]
            for h, block in enumerate(swap(*both)):
                r.wsep[2 * part + h, g, :, e * 128:(e + 1) * 128] = block.astype(BF)

    def lines(q, kk, v, u, same):
        lane_head = lax.broadcasted_iota(jnp.int32, (128, 256), 1) // 64

        def spread(a):
            return jnp.concatenate(
                [jnp.where(lane_head == h, a, jnp.zeros_like(a)) for h in range(4)], axis=0
            )

        qs, ks, vs, us = spread(q), spread(kk), spread(v), spread(u)
        s = dot_nt(q, ks)
        dp = dot_nt(u, vs)
        lows, dss = [], []
        for h in range(4):
            sj = jnp.where(same, s[:, h * 128:(h + 1) * 128] * SCALE, -1e30)
            e = jnp.exp(sj - jnp.max(sj, axis=-1, keepdims=True))
            pr = e / jnp.sum(e, axis=-1, keepdims=True)
            dpj = dp[:, h * 128:(h + 1) * 128]
            delta = jnp.sum(pr * dpj, axis=-1, keepdims=True)
            dss.append((pr * (dpj - delta) * SCALE).astype(BF))
            lows.append(pr.astype(BF))
        p_wide, ds_wide = jnp.concatenate(lows, axis=1), jnp.concatenate(dss, axis=1)
        p_tall, ds_tall = jnp.concatenate(lows, axis=0), jnp.concatenate(dss, axis=0)
        return dot(ds_wide, ks), dot_tn(ds_tall, qs), dot_tn(p_tall, us), dot(p_wide, vs)

    def blocks_of(a, b):
        pairs = [swap(a[:, e:e + 128], b[:, e:e + 128]) for e in (0, 128)]
        return jnp.concatenate([*pairs[0], *pairs[1]], axis=1).astype(BF)

    def home(first, count, g, same):
        normed = r.normed[first:first + count].reshape(count * 128, 768)
        c16 = r.c16[first:first + count].reshape(count * 128, 768)
        feats = [dot(normed, r.wsep[c, g]).astype(BF) for c in range(3)]
        feats.append(dot(c16, r.wsep[3, g]).astype(BF))
        grads = [[], [], []]
        for i in range(count):
            here = slice(i * 128, (i + 1) * 128)
            there = slice((first + i) * 128, (first + i + 1) * 128)
            gq, gk, gv, att = lines(*[a[here] for a in feats], same)
            r.gs_qk[g, there, :] = blocks_of(gq, gk)
            r.gs_v[g, there, :] = gv.astype(BF)
            r.gs_a[g, there, :] = att.astype(BF)
            for c, one in enumerate((gq, gk, gv)):
                grads[c].append(one.astype(BF))
        back = [dot_nt(jnp.concatenate(grads[c], axis=0), r.wsep[c, g]) for c in range(3)]
        back = (back[0] + back[1]) + back[2]
        for i in range(count):
            r.gn[first + i] += back[i * 128:(i + 1) * 128]

    @pl.loop(0, 2)
    def _(g):
        home(0, 1, g, row_i % 8 == col_i % 8)

    half = row_i // 64 == col_i // 64
    lines_arrived(0)
    prepare(1, r.xb[0].reshape(16, 16, 384))
    prepare(2, r.zb[0].reshape(16, 16, 384))
    lines_arrived(1)
    prepare_cotangent(1, r.xb[1].reshape(16, 16, 384))
    prepare_cotangent(2, r.zb[1].reshape(16, 16, 384))

    home(1, 2, 0, half)

    def weight_grad(part, g, dest):
        lhs = r.lt[0]
        if part == 0:
            full = dot(lhs, r.gs_qk[g])
            blocks = [full[:, e:e + 128] for e in range(0, 512, 128)]
        else:
            gv, ga = dot(lhs, r.gs_v[g]), dot(r.lt[1], r.gs_a[g])
            blocks = []
            for e in (0, 128):
                blocks.extend(swap(gv[:, e:e + 128], ga[:, e:e + 128]))
        for v in range(4):
            dest[g, v] = blocks[v].astype(dest.dtype)

    def to_other_core(g):
        for part in range(2):
            @pl.when(core == 1 - part)
            def _():
                weight_grad(part, g, r.gw_send)
        go("c", r.gw_send.at[g], r.gw_recv.at[g], g, g, pair)

    def own_part(g):
        for part in range(2):
            @pl.when(core == part)
            def _():
                weight_grad(part, g, r.gw_own)

    def four(ref):
        return (ref[0].astype(F32) + ref[1].astype(F32)) + (ref[2].astype(F32) + ref[3].astype(F32))

    def sum_first(g, between=lambda i: None):
        arrived("c", r.gw_recv.at[g], g, pair)
        for v in range(4):
            both = (r.gw_own[g, v] + r.gw_recv[g, v].astype(F32)).astype(BF).reshape(4, 4, 48, 128)
            r.a1s[g, v] = both[:2]
            for e in range(4):
                r.b1s[g, e, v] = both[2:, e]
        for i, d in enumerate((2, 1, 3)):
            between(i)
            v = (y + d) % 4
            go("a1", r.a1s.at[g, v], r.a1r.at[g, y], 4 * g + d, 4 * g + y, at_y(v))
            v = (x + d) % 4
            go("b1", r.b1s.at[g, j_of(v)], r.b1r.at[g, x], 4 * g + d, 4 * g + x, at_x(v))
        r.a1r[g, y] = r.a1s[g, y]
        r.b1r[g, x] = r.b1s[g, j]

    def sum_second(g):
        for d in range(1, 4):
            v = (y + d) % 4
            arrived("a1", r.a1r.at[g, v], 4 * g + v, at_y(v))
        a_sum = four(r.a1r.at[g]).astype(BF)
        for e in range(4):
            r.a2s[g, e] = a_sum[:, e]
        for d in (2, 1, 3):
            v = (x + d) % 4
            go("a2", r.a2s.at[g, j_of(v)], r.a2r.at[g, x], 4 * g + d, 4 * g + x, at_x(v))
        r.a2r[g, x] = r.a2s[g, j]
        for d in range(1, 4):
            v = (x + d) % 4
            arrived("b1", r.b1r.at[g, v], 4 * g + v, at_x(v))
        r.b2s[g] = four(r.b1r.at[g]).astype(BF)
        for d in (2, 1, 3):
            v = (y + d) % 4
            go("b2", r.b2s.at[g, v], r.b2r.at[g, y], 4 * g + d, 4 * g + y, at_y(v))
        r.b2r[g, y] = r.b2s[g, y]

    def z_copy(g, i):
        c = 8 * g + 2 * i + p
        return rcopy("z", r.zs.at[g, i], r.zr.at[z], 4 * g + i, z, at_z(c))

    def sum_third(g):
        for d in range(1, 4):
            v = (x + d) % 4
            arrived("a2", r.a2r.at[g, v], 4 * g + v, at_x(v))
        r.zs[g, 0:2] = four(r.a2r.at[g]).astype(BF)
        for d in range(1, 4):
            v = (y + d) % 4
            arrived("b2", r.b2r.at[g, v], 4 * g + v, at_y(v))
        r.zs[g, 2:4] = four(r.b2r.at[g]).astype(BF)

        @pl.loop(0, 4)
        def _(i):
            @pl.when(8 * g + 2 * i + p != z)
            def _():
                z_copy(g, i).start()

    home(1, 2, 1, half)

    g = r.gn[1]
    r.gx[...] = g.astype(BF).reshape(2, 4, 16, 768)
    for d in range(1, 4):
        v = (y + d) % 4
        go("gx", r.gx.at[:, v], r.xg.at[pl.ds(2 * y, 2)], d, y, at_y(v))
    r.xg[pl.ds(2 * y, 2)] = r.gx[:, y]
    g4 = r.gn[2].reshape(2, 8, 8, 768)
    r.gz[...] = jnp.concatenate([g4[0], g4[1]], axis=1).astype(BF)
    for d in range(1, 8):
        v = (k + d) % 8
        go("gz", r.gz.at[v], r.zg.at[k], d, k, at_k(v))
    r.zg[k] = r.gz[k]

    parts = [r.gn[0] * r.nrm[0] + r.gn[1] * r.nrm[1] + r.gn[2] * r.nrm[2], r.gn[0] + r.gn[1] + r.gn[2]]
    r.nk[k] = jnp.concatenate([jnp.sum(e, axis=0, keepdims=True) for e in parts], axis=0)
    for d in range(1, 8):
        go("nk", r.nk.at[k], r.nk.at[k], d, k, at_k((k + d) % 8))

    to_other_core(0)
    to_other_core(1)
    own_part(0)
    sum_first(0)
    own_part(1)

    for d in range(1, 8):
        v = (k + d) % 8
        arrived("nk", r.nk.at[v], v, at_k(v))
    both = r.nk[0]
    for v in range(1, 8):
        both = both + r.nk[v]
    r.ny[y] = jnp.where(core == 0, both[0:1], both[1:2])
    for d in range(1, 4):
        go("ny", r.ny.at[y], r.ny.at[y], d, y, at_y((y + d) % 4))

    for d in range(1, 4):
        v = (y + d) % 4
        arrived("gx", r.xg.at[pl.ds(2 * v, 2)], v, at_y(v))
    for d in range(1, 8):
        v = (k + d) % 8
        arrived("gz", r.zg.at[v], v, at_k(v))
    perm_g = one_hot(128, 128, lambda i: (i % 16) * 8 + i // 16)
    total = dot(perm_g, r.zg[...].reshape(128, 768)) + r.xg[...].reshape(128, 768).astype(F32)
    r.rb[...] = fold(total.reshape(16, 8, 768)).astype(BF).reshape(8, 2, 16, 384)

    def return_sends(i):
        @pl.loop(1 + 5 * i, 6 + 5 * i)
        def _(d):
            c = (z + d) % 16
            rcopy("rt", r.rb.at[c % 8, c // 8], r.ret.at[z], d, z, at_z(c)).start()

    for i in range(3):
        return_sends(i)
    sum_first(1)
    for d in range(1, 4):
        v = (y + d) % 4
        arrived("ny", r.ny.at[v], v, at_y(v))
    r.nz[z] = (r.ny[0] + r.ny[1]) + (r.ny[2] + r.ny[3])

    r.ret[z] = r.rb[z_lo, z_hi]

    @pl.loop(1, 16)
    def _(d):
        rcopy("nz", r.nz.at[z], r.nz.at[z], d, z, at_z((z + d) % 16)).start()

    sum_second(0)
    sum_second(1)

    sum_third(0)
    sum_third(1)

    @pl.when(holder)
    def _():
        r.zr[z] = r.zs[z_hi, z_lo // 2]

    @pl.loop(1, 16)
    def _(d):
        c = (z + d) % 16
        arrived("rt", r.ret.at[c], c, at_z(c))

    scaled = (r.gn[0] + unfold(r.ret[...])) * gain_row
    nrm = r.nrm[0]
    m1 = jnp.mean(scaled, axis=-1, keepdims=True)
    m2 = jnp.mean(scaled * nrm, axis=-1, keepdims=True)
    c_rows = r.c16[0].astype(F32)
    rows = (c_rows + r.inv_y[:, :1] * (scaled - m1 - nrm * m2)).astype(BF)
    perm_b = one_hot(128, 128, lambda i: (i % 16) * 8 + i // 16)
    r.tok_out[...] = dot(perm_b, rows).astype(BF)
    store_tok = pltpu.make_async_copy(r.tok_out, tok_res, lsem.at[5])
    store_tok.start()

    @pl.loop(1, 16)
    def _(d):
        c = (z + d) % 16
        arrived("nz", r.nz.at[c], c, at_z(c))

    row = r.nz[0]
    for c in range(1, 16):
        row = row + r.nz[c]
    r.norm_out[core] = row
    go("no", r.norm_out.at[core], r.norm_out.at[core], 0, core, pair)

    def final_copies():
        return [rcopy("f", r.qr.at[core], r.qr.at[core], d, core, quad(d)[1]) for d in range(1, 4)]

    @pl.when(holder)
    def _():
        @pl.loop(1, 16)
        def _(d):
            c = (z + d) % 16
            arrived("z", r.zr.at[c], c, at_z(c))

        z_total = r.zr[0].astype(F32)
        for c in range(1, 16):
            z_total = z_total + r.zr[c].astype(F32)
        r.qr[core] = z_total
        for copy in final_copies():
            copy.start()
        arrived("f", r.qr.at[1 - core], 1 - core, pair)

    @pl.when(jnp.logical_not(holder))
    def _():
        for d in range(2):
            arrived("f", r.qr.at[d], d, at_k((x + 1 - 2 * p) * 2 + d))

    arrived("no", r.norm_out.at[1 - core], 1 - core, pair)
    store_norm = pltpu.make_async_copy(r.norm_out, norm_res, lsem.at[6])
    store_norm.start()
    store_w = pltpu.make_async_copy(r.qr, w_res, lsem.at[7])
    store_w.start()

    for copy in sends:
        copy.wait_send()

    @pl.loop(1, 16)
    def _(d):
        c = (z + d) % 16
        dev = at_z(c)
        for e in range(2):
            token_copy(e, d).wait_send()
        rcopy("rt", r.rb.at[c % 8, c // 8], r.ret.at[z], d, z, dev).wait_send()
        rcopy("nz", r.nz.at[z], r.nz.at[z], d, z, dev).wait_send()

    for g in range(2):
        @pl.loop(0, 4)
        def _(i):
            @pl.when(8 * g + 2 * i + p != z)
            def _():
                z_copy(g, i).wait_send()

    @pl.when(holder)
    def _():
        @pl.loop(1, 16)
        def _(d):
            rcopy("wz", r.wpart.at[core], w_mine, d, z, at_z((z + d) % 16)).wait_send()

        for copy in final_copies():
            copy.wait_send()

    store_tok.wait()
    store_norm.wait()
    store_w.wait()


def per_device(tokens, cotangent, weights, norm_gain, norm_bias):
    scratch = list(BUFFERS.values())
    for count in SEMAPHORES.values():
        scratch += [pltpu.SemaphoreType.DMA((count,))] * 2
    scratch.append(pltpu.SemaphoreType.DMA((8,)))
    anywhere = pl.BlockSpec(memory_space=pltpu.HBM)
    grad_tok, grad_w, grad_norm = pl.pallas_call(
        kernel,
        out_shape=(
            jax.ShapeDtypeStruct((128, 768), BF),
            jax.ShapeDtypeStruct((2, 48, 128), F32),
            jax.ShapeDtypeStruct((2, 1, 768), F32),
        ),
        in_specs=[anywhere] * 5,
        out_specs=(anywhere,) * 3,
        scratch_shapes=scratch,
        compiler_params=pltpu.CompilerParams(
            collective_id=0, has_side_effects=True, vmem_limit_bytes=60 * 1024 * 1024
        ),
        name="axial_backward",
    )(tokens.reshape(128, 768), cotangent.reshape(128, 768), weights, norm_gain, norm_bias)
    member = lax.axis_index("slab") % 4
    mine = lax.dynamic_slice(grad_w, (0, member * 12, 0), (2, 12, 128))
    mine = mine.reshape(2, 12, 2, 64).transpose(1, 0, 2, 3).reshape(12, 4, 64)
    return grad_tok.reshape(tokens.shape), mine, grad_norm.reshape(2, 768)


def solution(mesh):
    return jax.shard_map(
        per_device,
        mesh=mesh,
        in_specs=(
            P("slab", "head", None, None),
            P("slab", "head", None, None),
            P("slab", None, "head"),
            P(),
            P(),
        ),
        out_specs=(P("slab", "head", None, None), P("slab", None, "head"), P()),
        check_vma=False,
    )
```

```python
import types

import jax
import jax.numpy as jnp
from jax import lax
from jax.experimental import pallas as pl
from jax.experimental.pallas import tpu as pltpu
from jax.sharding import PartitionSpec as P

MESH = pl.DeviceIdType.MESH
BF = jnp.bfloat16
F32 = jnp.float32
EPS = 1e-05
SCALE = 0.125
VM = pltpu.VMEM

BUFFERS = {
    "tok": VM((128, 768), BF),
    "cot": VM((128, 768), BF),
    "wraw": VM((12, 4, 64), BF),
    "gain": VM((768,), F32),
    "bias": VM((768,), F32),
    "wq": VM((4, 16, 256), BF),
    "wpart": VM((2, 48, 128), BF),
    "wb": VM((2, 2, 4, 4, 4, 48, 128), BF),
    "wsep": VM((4, 2, 768, 256), BF),
    "send_rows": VM((2, 16, 16, 384), BF),
    "p1": VM((2, 8, 2, 16, 384), BF),
    "xb": VM((2, 2, 4, 2, 16, 384), BF),
    "zv": VM((2, 8, 2, 16, 384), BF),
    "zb": VM((2, 2, 8, 16, 384), BF),
    "lt": VM((2, 768, 384), BF),
    "normed": VM((3, 128, 768), BF),
    "c16": VM((3, 128, 768), BF),
    "nrm": VM((3, 128, 768), F32),
    "gn": VM((3, 128, 768), F32),
    "gs_qk": VM((2, 384, 512), BF),
    "gs_v": VM((2, 384, 256), BF),
    "gs_a": VM((2, 384, 256), BF),
    "inv_y": VM((128, 128), F32),
    "gx": VM((2, 4, 16, 768), BF),
    "xg": VM((8, 16, 768), BF),
    "gz": VM((8, 16, 768), BF),
    "zg": VM((8, 16, 768), BF),
    "rb": VM((8, 2, 16, 384), BF),
    "ret": VM((16, 16, 384), BF),
    "gw_send": VM((2, 4, 768, 128), BF),
    "gw_recv": VM((2, 4, 768, 128), BF),
    "gw_own": VM((2, 4, 768, 128), F32),
    "a1s": VM((2, 4, 2, 4, 48, 128), BF),
    "a1r": VM((2, 4, 2, 4, 48, 128), BF),
    "b1s": VM((2, 4, 4, 2, 48, 128), BF),
    "b1r": VM((2, 4, 4, 2, 48, 128), BF),
    "a2s": VM((2, 4, 2, 48, 128), BF),
    "a2r": VM((2, 4, 2, 48, 128), BF),
    "b2s": VM((2, 4, 2, 48, 128), BF),
    "b2r": VM((2, 4, 2, 48, 128), BF),
    "zs": VM((2, 4, 48, 128), BF),
    "zr": VM((16, 48, 128), BF),
    "qr": VM((2, 48, 128), F32),
    "tok_out": VM((128, 768), BF),
    "norm_out": VM((2, 1, 768), F32),
    "nk": VM((8, 2, 768), F32),
    "ny": VM((4, 1, 768), F32),
    "nz": VM((16, 1, 768), F32),
}
SEMAPHORES = {
    "q": 4, "wz": 16, "wa1": 4, "wb1": 4, "wa2": 4, "wb2": 4, "wca": 4, "wcb": 4,
    "p1": 32, "xl": 8, "zl": 16, "gx": 4, "gz": 8, "rt": 16,
    "c": 2, "a1": 8, "b1": 8, "a2": 8, "b2": 8, "z": 16, "f": 4,
    "nk": 8, "ny": 4, "nz": 16, "no": 2,
}


def one_hot(rows, cols, source):
    dest = lax.broadcasted_iota(jnp.int32, (rows, cols), 0)
    src = lax.broadcasted_iota(jnp.int32, (rows, cols), 1)
    return (source(dest) == src).astype(BF)


def dot(a, b):
    return jnp.dot(a, b, preferred_element_type=F32)


def dot_nt(a, b):
    return lax.dot_general(a, b, (((1,), (1,)), ((), ())), preferred_element_type=F32)


def dot_tn(a, b):
    return lax.dot_general(a, b, (((0,), (0,)), ((), ())), preferred_element_type=F32)


def both_ways(i):
    return 8 + (1 - 2 * (i % 2)) * ((i + 1) // 2)


def fold(a):
    return jnp.concatenate([a[:, :, :384], a[:, :, 384:]], axis=1)


def unfold(a):
    a = a.astype(F32)
    return jnp.concatenate([a[:, :8], a[:, 8:]], axis=2).reshape(-1, 768)


def swap(a, b):
    low = lax.broadcasted_iota(jnp.int32, a.shape, 1) < 64
    return jnp.where(low, a, pltpu.roll(b, 64, 1)), jnp.where(low, pltpu.roll(a, 64, 1), b)


def kernel(tok_in, cot_in, w_in, gain_in, bias_in, tok_res, w_res, norm_res, *refs):
    names = list(BUFFERS)
    r = types.SimpleNamespace(**dict(zip(names, refs)))
    rest = refs[len(names):]
    ssem = {n: rest[2 * i] for i, n in enumerate(SEMAPHORES)}
    rsem = {n: rest[2 * i + 1] for i, n in enumerate(SEMAPHORES)}
    lsem = rest[-1]

    slab = lax.axis_index("slab")
    head = lax.axis_index("head")
    z_lo, x, core = slab // 8, (slab // 2) % 4, slab % 2
    y, z_hi = head // 2, head % 2
    z = z_hi * 8 + z_lo
    k = x * 2 + core
    p = x % 2
    j = 2 * p + x // 2
    member = p * 2 + core
    holder = z_lo % 2 == p

    def at_z(c):
        return ((c % 8) * 8 + k, y * 2 + c // 8)

    def at_y(v):
        return (slab, v * 2 + z_hi)

    def at_k(v):
        return (z_lo * 8 + v, head)

    def at_x(v):
        return at_k(v * 2 + core)

    def j_of(v):
        return 2 * (v % 2) + v // 2

    pair = at_k(x * 2 + 1 - core)

    def rcopy(name, src, dst, si, ri, dev):
        return pltpu.make_async_remote_copy(
            src_ref=src, dst_ref=dst, send_sem=ssem[name].at[si], recv_sem=rsem[name].at[ri],
            device_id=dev, device_id_type=MESH,
        )

    sends = []

    def go(*args):
        copy = rcopy(*args)
        copy.start()
        sends.append(copy)

    def arrived(name, dst, ri, dev):
        rcopy(name, dst, dst, 0, ri, dev).wait_recv()

    loads = [
        pltpu.make_async_copy(src, dst, lsem.at[i])
        for i, (src, dst) in enumerate(
            ((w_in, r.wraw), (tok_in, r.tok), (cot_in, r.cot), (gain_in, r.gain), (bias_in, r.bias))
        )
    ]
    for load in loads:
        load.start()

    barrier = pltpu.get_barrier_semaphore()

    @pl.loop(1, 16)
    def _(d):
        pl.semaphore_signal(barrier, inc=1, device_id=at_z((z + d) % 16), device_id_type=MESH)

    for d in range(1, 4):
        pl.semaphore_signal(barrier, inc=1, device_id=at_y((y + d) % 4), device_id_type=MESH)
    for d in range(1, 8):
        pl.semaphore_signal(barrier, inc=1, device_id=at_k((k + d) % 8), device_id_type=MESH)

    loads[0].wait()
    wide = jnp.concatenate([r.wraw[:, c, :].astype(F32) for c in range(4)], axis=1)
    wide = jnp.concatenate([wide, jnp.zeros((4, 256), F32)], axis=0)
    r.wq[member] = wide.astype(BF)
    pl.semaphore_wait(barrier, 25)

    def quad(d):
        other = (member + d) % 4
        return other, at_k(((other // 2) + 2 * (x // 2)) * 2 + other % 2)

    for d in range(1, 4):
        other, dev = quad(d)
        go("q", r.wq.at[member], r.wq.at[member], d, member, dev)

    for load in loads[1:]:
        load.wait()

    perm = one_hot(128, 128, lambda i: (i % 8) * 16 + i // 8)
    for e, ref in enumerate((r.tok, r.cot)):
        r.send_rows[e] = fold(dot(perm, ref[...]).reshape(16, 8, 768)).astype(BF)

    def token_copy(e, d):
        c = (z + d) % 16
        return rcopy("p1", r.send_rows.at[e, c], r.p1.at[e, z_lo, z_hi], 16 * e + d, 16 * e + z, at_z(c))

    def token_sends(e, start, stop):
        @pl.loop(start, stop)
        def _(i):
            token_copy(e, both_ways(i)).start()

    token_sends(0, 0, 3)

    gain_row, bias_row = r.gain[...].reshape(1, 768), r.bias[...].reshape(1, 768)

    def prepare_cotangent(idx, rows):
        c16 = unfold(rows).astype(BF)
        r.lt[1, :, idx * 128:(idx + 1) * 128] = c16.T
        r.c16[idx] = c16

    def prepare(idx, rows):
        here = slice(idx * 128, (idx + 1) * 128)
        t = unfold(rows)
        centred = t - jnp.mean(t, axis=-1, keepdims=True)
        inv = lax.rsqrt(jnp.mean(centred * centred, axis=-1, keepdims=True) + EPS)
        nrm = centred * inv
        normed = (nrm * gain_row + bias_row).astype(BF)
        r.lt[0, :, here] = normed.T
        r.normed[idx] = normed
        r.nrm[idx] = nrm
        r.gn[idx] = jnp.zeros((128, 768), F32)
        return inv

    for d in range(1, 4):
        other, dev = quad(d)
        arrived("q", r.wq.at[other], other, dev)
    stack = one_hot(48, 64, lambda i: (i // 12) * 16 + i % 12)
    block = dot(stack, r.wq[...].reshape(64, 256)).astype(BF)
    r.wpart[0] = block[:, :128]
    r.wpart[1] = block[:, 128:]

    w_mine = r.wb.at[core, z_hi, y, z_lo // 2, j]

    @pl.when(holder)
    def _():
        w_mine[...] = r.wpart[core]

        @pl.loop(0, 15)
        def _(i):
            d = both_ways(i)
            rcopy("wz", r.wpart.at[core], w_mine, d, z, at_z((z + d) % 16)).start()

    r.inv_y[...] = jnp.broadcast_to(prepare(0, r.send_rows[0]), (128, 128))
    prepare_cotangent(0, r.send_rows[1])

    @pl.loop(0, 8)
    def _(i):
        c = 2 * i + p

        @pl.when(c != z)
        def _():
            arrived("wz", r.wb.at[core, c // 8, y, (c % 8) // 2, j], c, at_z(c))

    def w_a(v):
        return r.wb.at[core, 0, y, :, j_of(v)]

    def w_b(v):
        return r.wb.at[core, 1, v, :, j]

    for d in range(1, 4):
        go("wa1", w_a(x), w_a(x), d, x, at_x((x + d) % 4))
        go("wb1", w_b(y), w_b(y), d, y, at_y((y + d) % 4))
    token_sends(0, 3, 8)
    for e in range(2):
        r.p1[e, z_lo, z_hi] = r.send_rows[e, z]

    for d in range(1, 4):
        v = (x + d) % 4
        arrived("wa1", w_a(v), v, at_x(v))
    a_mine, b_mine = r.wb.at[core, 0, y], r.wb.at[core, 1, :, :, j]
    go("wca", a_mine, a_mine, 0, y, pair)
    for d, span in ((1, (8, 10)), (3, (10, 12)), (2, (12, 15))):
        go("wa2", a_mine, a_mine, d, y, at_y((y + d) % 4))
        token_sends(0, *span)
    for d in range(1, 4):
        v = (y + d) % 4
        arrived("wb1", w_b(v), v, at_y(v))
    go("wcb", b_mine, b_mine, 0, x, pair)
    for d, span in ((1, (0, 4)), (3, (4, 8)), (2, (8, 15))):
        go("wb2", b_mine, b_mine, d, x, at_x((x + d) % 4))
        token_sends(1, *span)

    perm_v = one_hot(
        256, 256, lambda i: (i % 8) * 32 + (i // 128) * 16 + ((i // 8) % 2) * 8 + (i // 16) % 8
    )

    def second_hop(e):
        @pl.loop(1, 16)
        def _(d):
            c = (z + d) % 16
            arrived("p1", r.p1.at[e, c % 8, c // 8], 16 * e + c, at_z(c))

        for d in range(1, 4):
            v = (y + d) % 4
            go("xl", r.p1.at[e, pl.ds(2 * v, 2)], r.xb.at[e, :, y], 4 * e + d, 4 * e + y, at_y(v))
        r.xb[e, :, y] = r.p1[e, pl.ds(2 * y, 2)]
        r.zv[e] = dot(perm_v, r.p1[e].reshape(256, 384)).astype(BF).reshape(8, 2, 16, 384)
        for d in range(1, 8):
            v = (k + d) % 8
            go("zl", r.zv.at[e, v], r.zb.at[e, :, k], 8 * e + d, 8 * e + k, at_k(v))
        r.zb[e, :, k] = r.zv[e, k]

    def lines_arrived(e):
        for d in range(1, 4):
            v = (y + d) % 4
            arrived("xl", r.xb.at[e, :, v], 4 * e + v, at_y(v))
        for d in range(1, 8):
            v = (k + d) % 8
            arrived("zl", r.zb.at[e, :, v], 8 * e + v, at_k(v))

    second_hop(0)

    for d in (1, 3, 2):
        v = (y + d) % 4
        theirs = r.wb.at[core, 0, v]
        arrived("wa2", theirs, v, at_y(v))
        go("wca", theirs, theirs, d, v, pair)
        v = (x + d) % 4
        theirs = r.wb.at[core, 1, :, :, j_of(v)]
        arrived("wb2", theirs, v, at_x(v))
        go("wcb", theirs, theirs, d, v, pair)
    def separate(part):
        @pl.loop(0, 2)
        def _(g):
            for e in range(2):
                both = [r.wb[part, g, 2 * e + h].reshape(768, 128).astype(F32) for h in range(2)]
                for h, block in enumerate(swap(*both)):
                    r.wsep[2 * part + h, g, :, e * 128:(e + 1) * 128] = block.astype(BF)

    second_hop(1)
    separate(core)

    for d in range(4):
        v = (y + d) % 4
        arrived("wca", r.wb.at[1 - core, 0, v], v, pair)
        v = (x + d) % 4
        arrived("wcb", r.wb.at[1 - core, 1, :, :, j_of(v)], v, pair)

    separate(1 - core)

    row_i = lax.broadcasted_iota(jnp.int32, (128, 128), 0)
    col_i = lax.broadcasted_iota(jnp.int32, (128, 128), 1)

    def lines(q, kk, v, u, same):
        lane_head = lax.broadcasted_iota(jnp.int32, (128, 256), 1) // 64

        def spread(a):
            return jnp.concatenate(
                [jnp.where(lane_head == h, a, jnp.zeros_like(a)) for h in range(4)], axis=0
            )

        qs, ks, vs, us = spread(q), spread(kk), spread(v), spread(u)
        s = dot_nt(q, ks)
        dp = dot_nt(u, vs)
        lows, dss = [], []
        for h in range(4):
            sj = jnp.where(same, s[:, h * 128:(h + 1) * 128] * SCALE, -1e30)
            e = jnp.exp(sj - jnp.max(sj, axis=-1, keepdims=True))
            pr = e / jnp.sum(e, axis=-1, keepdims=True)
            dpj = dp[:, h * 128:(h + 1) * 128]
            delta = jnp.sum(pr * dpj, axis=-1, keepdims=True)
            dss.append((pr * (dpj - delta) * SCALE).astype(BF))
            lows.append(pr.astype(BF))
        p_wide, ds_wide = jnp.concatenate(lows, axis=1), jnp.concatenate(dss, axis=1)
        p_tall, ds_tall = jnp.concatenate(lows, axis=0), jnp.concatenate(dss, axis=0)
        return dot(ds_wide, ks), dot_tn(ds_tall, qs), dot_tn(p_tall, us), dot(p_wide, vs)

    def blocks_of(a, b):
        pairs = [swap(a[:, e:e + 128], b[:, e:e + 128]) for e in (0, 128)]
        return jnp.concatenate([*pairs[0], *pairs[1]], axis=1).astype(BF)

    def home(first, count, g, same):
        normed = r.normed[first:first + count].reshape(count * 128, 768)
        c16 = r.c16[first:first + count].reshape(count * 128, 768)
        feats = [dot(normed, r.wsep[c, g]).astype(BF) for c in range(3)]
        feats.append(dot(c16, r.wsep[3, g]).astype(BF))
        grads = [[], [], []]
        for i in range(count):
            here = slice(i * 128, (i + 1) * 128)
            there = slice((first + i) * 128, (first + i + 1) * 128)
            gq, gk, gv, att = lines(*[a[here] for a in feats], same)
            r.gs_qk[g, there, :] = blocks_of(gq, gk)
            r.gs_v[g, there, :] = gv.astype(BF)
            r.gs_a[g, there, :] = att.astype(BF)
            for c, one in enumerate((gq, gk, gv)):
                grads[c].append(one.astype(BF))
        back = [dot_nt(jnp.concatenate(grads[c], axis=0), r.wsep[c, g]) for c in range(3)]
        back = (back[0] + back[1]) + back[2]
        for i in range(count):
            r.gn[first + i] += back[i * 128:(i + 1) * 128]

    @pl.loop(0, 2)
    def _(g):
        home(0, 1, g, row_i % 8 == col_i % 8)

    half = row_i // 64 == col_i // 64
    lines_arrived(0)
    prepare(1, r.xb[0].reshape(16, 16, 384))
    prepare(2, r.zb[0].reshape(16, 16, 384))
    lines_arrived(1)
    prepare_cotangent(1, r.xb[1].reshape(16, 16, 384))
    prepare_cotangent(2, r.zb[1].reshape(16, 16, 384))

    home(1, 2, 0, half)

    def weight_grad(part, g, dest):
        lhs = r.lt[0]
        if part == 0:
            full = dot(lhs, r.gs_qk[g])
            blocks = [full[:, e:e + 128] for e in range(0, 512, 128)]
        else:
            gv, ga = dot(lhs, r.gs_v[g]), dot(r.lt[1], r.gs_a[g])
            blocks = []
            for e in (0, 128):
                blocks.extend(swap(gv[:, e:e + 128], ga[:, e:e + 128]))
        for v in range(4):
            dest[g, v] = blocks[v].astype(dest.dtype)

    def to_other_core(g):
        for part in range(2):
            @pl.when(core == 1 - part)
            def _():
                weight_grad(part, g, r.gw_send)
        go("c", r.gw_send.at[g], r.gw_recv.at[g], g, g, pair)

    def own_part(g):
        for part in range(2):
            @pl.when(core == part)
            def _():
                weight_grad(part, g, r.gw_own)

    def four(ref):
        return (ref[0].astype(F32) + ref[1].astype(F32)) + (ref[2].astype(F32) + ref[3].astype(F32))

    def sum_first(g, between=lambda i: None):
        arrived("c", r.gw_recv.at[g], g, pair)
        for v in range(4):
            both = (r.gw_own[g, v] + r.gw_recv[g, v].astype(F32)).astype(BF).reshape(4, 4, 48, 128)
            r.a1s[g, v] = both[:2]
            for e in range(4):
                r.b1s[g, e, v] = both[2:, e]
        for i, d in enumerate((2, 1, 3)):
            between(i)
            v = (y + d) % 4
            go("a1", r.a1s.at[g, v], r.a1r.at[g, y], 4 * g + d, 4 * g + y, at_y(v))
            v = (x + d) % 4
            go("b1", r.b1s.at[g, j_of(v)], r.b1r.at[g, x], 4 * g + d, 4 * g + x, at_x(v))
        r.a1r[g, y] = r.a1s[g, y]
        r.b1r[g, x] = r.b1s[g, j]

    def sum_second(g):
        for d in range(1, 4):
            v = (y + d) % 4
            arrived("a1", r.a1r.at[g, v], 4 * g + v, at_y(v))
        a_sum = four(r.a1r.at[g]).astype(BF)
        for e in range(4):
            r.a2s[g, e] = a_sum[:, e]
        for d in (2, 1, 3):
            v = (x + d) % 4
            go("a2", r.a2s.at[g, j_of(v)], r.a2r.at[g, x], 4 * g + d, 4 * g + x, at_x(v))
        r.a2r[g, x] = r.a2s[g, j]
        for d in range(1, 4):
            v = (x + d) % 4
            arrived("b1", r.b1r.at[g, v], 4 * g + v, at_x(v))
        r.b2s[g] = four(r.b1r.at[g]).astype(BF)
        for d in (2, 1, 3):
            v = (y + d) % 4
            go("b2", r.b2s.at[g, v], r.b2r.at[g, y], 4 * g + d, 4 * g + y, at_y(v))
        r.b2r[g, y] = r.b2s[g, y]

    def z_copy(g, i):
        c = 8 * g + 2 * i + p
        return rcopy("z", r.zs.at[g, i], r.zr.at[z], 4 * g + i, z, at_z(c))

    def sum_third(g):
        for d in range(1, 4):
            v = (x + d) % 4
            arrived("a2", r.a2r.at[g, v], 4 * g + v, at_x(v))
        r.zs[g, 0:2] = four(r.a2r.at[g]).astype(BF)
        for d in range(1, 4):
            v = (y + d) % 4
            arrived("b2", r.b2r.at[g, v], 4 * g + v, at_y(v))
        r.zs[g, 2:4] = four(r.b2r.at[g]).astype(BF)

        @pl.loop(0, 4)
        def _(i):
            @pl.when(8 * g + 2 * i + p != z)
            def _():
                z_copy(g, i).start()

    home(1, 2, 1, half)

    g = r.gn[1]
    r.gx[...] = g.astype(BF).reshape(2, 4, 16, 768)
    for d in range(1, 4):
        v = (y + d) % 4
        go("gx", r.gx.at[:, v], r.xg.at[pl.ds(2 * y, 2)], d, y, at_y(v))
    r.xg[pl.ds(2 * y, 2)] = r.gx[:, y]
    g4 = r.gn[2].reshape(2, 8, 8, 768)
    r.gz[...] = jnp.concatenate([g4[0], g4[1]], axis=1).astype(BF)
    for d in range(1, 8):
        v = (k + d) % 8
        go("gz", r.gz.at[v], r.zg.at[k], d, k, at_k(v))
    r.zg[k] = r.gz[k]

    parts = [r.gn[0] * r.nrm[0] + r.gn[1] * r.nrm[1] + r.gn[2] * r.nrm[2], r.gn[0] + r.gn[1] + r.gn[2]]
    r.nk[k] = jnp.concatenate([jnp.sum(e, axis=0, keepdims=True) for e in parts], axis=0)
    for d in range(1, 8):
        go("nk", r.nk.at[k], r.nk.at[k], d, k, at_k((k + d) % 8))

    to_other_core(0)
    to_other_core(1)
    own_part(0)
    sum_first(0)
    own_part(1)

    for d in range(1, 8):
        v = (k + d) % 8
        arrived("nk", r.nk.at[v], v, at_k(v))
    both = r.nk[0]
    for v in range(1, 8):
        both = both + r.nk[v]
    r.ny[y] = jnp.where(core == 0, both[0:1], both[1:2])
    for d in range(1, 4):
        go("ny", r.ny.at[y], r.ny.at[y], d, y, at_y((y + d) % 4))

    for d in range(1, 4):
        v = (y + d) % 4
        arrived("gx", r.xg.at[pl.ds(2 * v, 2)], v, at_y(v))
    for d in range(1, 8):
        v = (k + d) % 8
        arrived("gz", r.zg.at[v], v, at_k(v))
    perm_g = one_hot(128, 128, lambda i: (i % 16) * 8 + i // 16)
    total = dot(perm_g, r.zg[...].reshape(128, 768)) + r.xg[...].reshape(128, 768).astype(F32)
    r.rb[...] = fold(total.reshape(16, 8, 768)).astype(BF).reshape(8, 2, 16, 384)

    def return_sends(i):
        @pl.loop(5 * i, 5 * i + 5)
        def _(n):
            d = both_ways(n)
            c = (z + d) % 16
            rcopy("rt", r.rb.at[c % 8, c // 8], r.ret.at[z], d, z, at_z(c)).start()

    for i in range(3):
        return_sends(i)
    sum_first(1)
    for d in range(1, 4):
        v = (y + d) % 4
        arrived("ny", r.ny.at[v], v, at_y(v))
    r.nz[z] = (r.ny[0] + r.ny[1]) + (r.ny[2] + r.ny[3])

    r.ret[z] = r.rb[z_lo, z_hi]

    @pl.loop(0, 15)
    def _(i):
        d = both_ways(i)
        rcopy("nz", r.nz.at[z], r.nz.at[z], d, z, at_z((z + d) % 16)).start()

    sum_second(0)
    sum_second(1)

    sum_third(0)
    sum_third(1)

    @pl.when(holder)
    def _():
        r.zr[z] = r.zs[z_hi, z_lo // 2]

    @pl.loop(1, 16)
    def _(d):
        c = (z + d) % 16
        arrived("rt", r.ret.at[c], c, at_z(c))

    scaled = (r.gn[0] + unfold(r.ret[...])) * gain_row
    nrm = r.nrm[0]
    m1 = jnp.mean(scaled, axis=-1, keepdims=True)
    m2 = jnp.mean(scaled * nrm, axis=-1, keepdims=True)
    c_rows = r.c16[0].astype(F32)
    rows = (c_rows + r.inv_y[:, :1] * (scaled - m1 - nrm * m2)).astype(BF)
    perm_b = one_hot(128, 128, lambda i: (i % 16) * 8 + i // 16)
    r.tok_out[...] = dot(perm_b, rows).astype(BF)
    store_tok = pltpu.make_async_copy(r.tok_out, tok_res, lsem.at[5])
    store_tok.start()

    @pl.loop(1, 16)
    def _(d):
        c = (z + d) % 16
        arrived("nz", r.nz.at[c], c, at_z(c))

    row = r.nz[0]
    for c in range(1, 16):
        row = row + r.nz[c]
    r.norm_out[core] = row
    go("no", r.norm_out.at[core], r.norm_out.at[core], 0, core, pair)

    def final_copies():
        return [rcopy("f", r.qr.at[core], r.qr.at[core], d, core, quad(d)[1]) for d in range(1, 4)]

    @pl.when(holder)
    def _():
        @pl.loop(1, 16)
        def _(d):
            c = (z + d) % 16
            arrived("z", r.zr.at[c], c, at_z(c))

        z_total = r.zr[0].astype(F32)
        for c in range(1, 16):
            z_total = z_total + r.zr[c].astype(F32)
        r.qr[core] = z_total
        for copy in final_copies():
            copy.start()
        arrived("f", r.qr.at[1 - core], 1 - core, pair)

    @pl.when(jnp.logical_not(holder))
    def _():
        for d in range(2):
            arrived("f", r.qr.at[d], d, at_k((x + 1 - 2 * p) * 2 + d))

    arrived("no", r.norm_out.at[1 - core], 1 - core, pair)
    store_norm = pltpu.make_async_copy(r.norm_out, norm_res, lsem.at[6])
    store_norm.start()
    store_w = pltpu.make_async_copy(r.qr, w_res, lsem.at[7])
    store_w.start()

    for copy in sends:
        copy.wait_send()

    @pl.loop(1, 16)
    def _(d):
        c = (z + d) % 16
        dev = at_z(c)
        for e in range(2):
            token_copy(e, d).wait_send()
        rcopy("rt", r.rb.at[c % 8, c // 8], r.ret.at[z], d, z, dev).wait_send()
        rcopy("nz", r.nz.at[z], r.nz.at[z], d, z, dev).wait_send()

    for g in range(2):
        @pl.loop(0, 4)
        def _(i):
            @pl.when(8 * g + 2 * i + p != z)
            def _():
                z_copy(g, i).wait_send()

    @pl.when(holder)
    def _():
        @pl.loop(1, 16)
        def _(d):
            rcopy("wz", r.wpart.at[core], w_mine, d, z, at_z((z + d) % 16)).wait_send()

        for copy in final_copies():
            copy.wait_send()

    store_tok.wait()
    store_norm.wait()
    store_w.wait()


def per_device(tokens, cotangent, weights, norm_gain, norm_bias):
    scratch = list(BUFFERS.values())
    for count in SEMAPHORES.values():
        scratch += [pltpu.SemaphoreType.DMA((count,))] * 2
    scratch.append(pltpu.SemaphoreType.DMA((8,)))
    anywhere = pl.BlockSpec(memory_space=pltpu.HBM)
    grad_tok, grad_w, grad_norm = pl.pallas_call(
        kernel,
        out_shape=(
            jax.ShapeDtypeStruct((128, 768), BF),
            jax.ShapeDtypeStruct((2, 48, 128), F32),
            jax.ShapeDtypeStruct((2, 1, 768), F32),
        ),
        in_specs=[anywhere] * 5,
        out_specs=(anywhere,) * 3,
        scratch_shapes=scratch,
        compiler_params=pltpu.CompilerParams(
            collective_id=0, has_side_effects=True, vmem_limit_bytes=60 * 1024 * 1024
        ),
        name="axial_backward",
    )(tokens.reshape(128, 768), cotangent.reshape(128, 768), weights, norm_gain, norm_bias)
    member = lax.axis_index("slab") % 4
    mine = lax.dynamic_slice(grad_w, (0, member * 12, 0), (2, 12, 128))
    mine = mine.reshape(2, 12, 2, 64).transpose(1, 0, 2, 3).reshape(12, 4, 64)
    return grad_tok.reshape(tokens.shape), mine, grad_norm.reshape(2, 768)


def solution(mesh):
    return jax.shard_map(
        per_device,
        mesh=mesh,
        in_specs=(
            P("slab", "head", None, None),
            P("slab", "head", None, None),
            P("slab", None, "head"),
            P(),
            P(),
        ),
        out_specs=(P("slab", "head", None, None), P("slab", None, "head"), P()),
        check_vma=False,
    )
```

```python
import types

import jax
import jax.numpy as jnp
from jax import lax
from jax.experimental import pallas as pl
from jax.experimental.pallas import tpu as pltpu
from jax.sharding import PartitionSpec as P

MESH = pl.DeviceIdType.MESH
BF = jnp.bfloat16
F32 = jnp.float32
EPS = 1e-05
SCALE = 0.125
VM = pltpu.VMEM

BUFFERS = {
    "tok": VM((128, 768), BF),
    "cot": VM((128, 768), BF),
    "wraw": VM((12, 4, 64), BF),
    "gain": VM((768,), F32),
    "bias": VM((768,), F32),
    "wq": VM((4, 16, 256), BF),
    "wpart": VM((2, 48, 128), BF),
    "wb": VM((2, 2, 4, 4, 4, 48, 128), BF),
    "wsep": VM((4, 2, 768, 256), BF),
    "send_rows": VM((2, 16, 16, 384), BF),
    "p1": VM((2, 8, 2, 16, 384), BF),
    "xb": VM((2, 2, 4, 2, 16, 384), BF),
    "zv": VM((2, 8, 2, 16, 384), BF),
    "zb": VM((2, 2, 8, 16, 384), BF),
    "lt": VM((2, 768, 384), BF),
    "normed": VM((3, 128, 768), BF),
    "c16": VM((3, 128, 768), BF),
    "nrm": VM((3, 128, 768), F32),
    "gn": VM((3, 128, 768), F32),
    "gs_qk": VM((2, 384, 512), BF),
    "gs_v": VM((2, 384, 256), BF),
    "gs_a": VM((2, 384, 256), BF),
    "inv_y": VM((128, 128), F32),
    "gx": VM((2, 4, 16, 768), BF),
    "xg": VM((8, 16, 768), BF),
    "gz": VM((8, 16, 768), BF),
    "zg": VM((8, 16, 768), BF),
    "rb": VM((8, 2, 16, 384), BF),
    "ret": VM((16, 16, 384), BF),
    "gw_send": VM((2, 4, 768, 128), BF),
    "gw_recv": VM((2, 4, 768, 128), BF),
    "gw_own": VM((2, 4, 768, 128), F32),
    "a1s": VM((2, 4, 2, 4, 48, 128), BF),
    "a1r": VM((2, 4, 2, 4, 48, 128), BF),
    "b1s": VM((2, 4, 4, 2, 48, 128), BF),
    "b1r": VM((2, 4, 4, 2, 48, 128), BF),
    "a2s": VM((2, 4, 2, 48, 128), BF),
    "a2r": VM((2, 4, 2, 48, 128), BF),
    "b2s": VM((2, 4, 2, 48, 128), BF),
    "b2r": VM((2, 4, 2, 48, 128), BF),
    "zs": VM((2, 4, 48, 128), BF),
    "zr": VM((16, 48, 128), BF),
    "qr": VM((2, 48, 128), F32),
    "tok_out": VM((128, 768), BF),
    "norm_out": VM((2, 1, 768), F32),
    "nk": VM((8, 2, 768), F32),
    "ny": VM((4, 1, 768), F32),
    "nz": VM((16, 1, 768), F32),
}
SEMAPHORES = {
    "q": 4, "wz": 16, "wa1": 4, "wb1": 4, "wa2": 8, "wb2": 8, "wca": 8, "wcb": 8,
    "p1": 32, "xl": 8, "zl": 16, "gx": 4, "gz": 8, "rt": 16,
    "c": 2, "a1": 8, "b1": 8, "a2": 8, "b2": 8, "z": 16, "f": 4,
    "nk": 8, "ny": 4, "nz": 16, "no": 2,
}


def one_hot(rows, cols, source):
    dest = lax.broadcasted_iota(jnp.int32, (rows, cols), 0)
    src = lax.broadcasted_iota(jnp.int32, (rows, cols), 1)
    return (source(dest) == src).astype(BF)


def dot(a, b):
    return jnp.dot(a, b, preferred_element_type=F32)


def dot_nt(a, b):
    return lax.dot_general(a, b, (((1,), (1,)), ((), ())), preferred_element_type=F32)


def dot_tn(a, b):
    return lax.dot_general(a, b, (((0,), (0,)), ((), ())), preferred_element_type=F32)


def both_ways(i):
    return 8 + (1 - 2 * (i % 2)) * ((i + 1) // 2)


def fold(a):
    return jnp.concatenate([a[:, :, :384], a[:, :, 384:]], axis=1)


def unfold(a):
    a = a.astype(F32)
    return jnp.concatenate([a[:, :8], a[:, 8:]], axis=2).reshape(-1, 768)


def swap(a, b):
    low = lax.broadcasted_iota(jnp.int32, a.shape, 1) < 64
    return jnp.where(low, a, pltpu.roll(b, 64, 1)), jnp.where(low, pltpu.roll(a, 64, 1), b)


def kernel(tok_in, cot_in, w_in, gain_in, bias_in, tok_res, w_res, norm_res, *refs):
    names = list(BUFFERS)
    r = types.SimpleNamespace(**dict(zip(names, refs)))
    rest = refs[len(names):]
    ssem = {n: rest[2 * i] for i, n in enumerate(SEMAPHORES)}
    rsem = {n: rest[2 * i + 1] for i, n in enumerate(SEMAPHORES)}
    lsem = rest[-1]

    slab = lax.axis_index("slab")
    head = lax.axis_index("head")
    z_lo, x, core = slab // 8, (slab // 2) % 4, slab % 2
    y, z_hi = head // 2, head % 2
    z = z_hi * 8 + z_lo
    k = x * 2 + core
    p = x % 2
    j = 2 * p + x // 2
    member = p * 2 + core
    holder = z_lo % 2 == p

    def at_z(c):
        return ((c % 8) * 8 + k, y * 2 + c // 8)

    def at_y(v):
        return (slab, v * 2 + z_hi)

    def at_k(v):
        return (z_lo * 8 + v, head)

    def at_x(v):
        return at_k(v * 2 + core)

    def j_of(v):
        return 2 * (v % 2) + v // 2

    pair = at_k(x * 2 + 1 - core)

    def rcopy(name, src, dst, si, ri, dev):
        return pltpu.make_async_remote_copy(
            src_ref=src, dst_ref=dst, send_sem=ssem[name].at[si], recv_sem=rsem[name].at[ri],
            device_id=dev, device_id_type=MESH,
        )

    sends = []

    def go(*args):
        copy = rcopy(*args)
        copy.start()
        sends.append(copy)

    def arrived(name, dst, ri, dev):
        rcopy(name, dst, dst, 0, ri, dev).wait_recv()

    loads = [
        pltpu.make_async_copy(src, dst, lsem.at[i])
        for i, (src, dst) in enumerate(
            ((w_in, r.wraw), (tok_in, r.tok), (cot_in, r.cot), (gain_in, r.gain), (bias_in, r.bias))
        )
    ]
    for load in loads:
        load.start()

    barrier = pltpu.get_barrier_semaphore()

    @pl.loop(1, 16)
    def _(d):
        pl.semaphore_signal(barrier, inc=1, device_id=at_z((z + d) % 16), device_id_type=MESH)

    for d in range(1, 4):
        pl.semaphore_signal(barrier, inc=1, device_id=at_y((y + d) % 4), device_id_type=MESH)
    for d in range(1, 8):
        pl.semaphore_signal(barrier, inc=1, device_id=at_k((k + d) % 8), device_id_type=MESH)

    loads[0].wait()
    wide = jnp.concatenate([r.wraw[:, c, :].astype(F32) for c in range(4)], axis=1)
    wide = jnp.concatenate([wide, jnp.zeros((4, 256), F32)], axis=0)
    r.wq[member] = wide.astype(BF)
    pl.semaphore_wait(barrier, 25)

    def quad(d):
        other = (member + d) % 4
        return other, at_k(((other // 2) + 2 * (x // 2)) * 2 + other % 2)

    for d in range(1, 4):
        other, dev = quad(d)
        go("q", r.wq.at[member], r.wq.at[member], d, member, dev)

    for load in loads[1:]:
        load.wait()

    perm = one_hot(128, 128, lambda i: (i % 8) * 16 + i // 8)
    for e, ref in enumerate((r.tok, r.cot)):
        r.send_rows[e] = fold(dot(perm, ref[...]).reshape(16, 8, 768)).astype(BF)

    def token_copy(e, d):
        c = (z + d) % 16
        return rcopy("p1", r.send_rows.at[e, c], r.p1.at[e, z_lo, z_hi], 16 * e + d, 16 * e + z, at_z(c))

    def token_sends(e, start, stop):
        @pl.loop(start, stop)
        def _(i):
            token_copy(e, both_ways(i)).start()

    token_sends(0, 0, 3)

    gain_row, bias_row = r.gain[...].reshape(1, 768), r.bias[...].reshape(1, 768)

    def prepare_cotangent(idx, rows):
        c16 = unfold(rows).astype(BF)
        r.lt[1, :, idx * 128:(idx + 1) * 128] = c16.T
        r.c16[idx] = c16

    def prepare(idx, rows):
        here = slice(idx * 128, (idx + 1) * 128)
        t = unfold(rows)
        centred = t - jnp.mean(t, axis=-1, keepdims=True)
        inv = lax.rsqrt(jnp.mean(centred * centred, axis=-1, keepdims=True) + EPS)
        nrm = centred * inv
        normed = (nrm * gain_row + bias_row).astype(BF)
        r.lt[0, :, here] = normed.T
        r.normed[idx] = normed
        r.nrm[idx] = nrm
        r.gn[idx] = jnp.zeros((128, 768), F32)
        return inv

    for d in range(1, 4):
        other, dev = quad(d)
        arrived("q", r.wq.at[other], other, dev)
    stack = one_hot(48, 64, lambda i: (i // 12) * 16 + i % 12)
    block = dot(stack, r.wq[...].reshape(64, 256)).astype(BF)
    r.wpart[0] = block[:, :128]
    r.wpart[1] = block[:, 128:]

    w_mine = r.wb.at[core, z_hi, y, z_lo // 2, j]

    @pl.when(holder)
    def _():
        w_mine[...] = r.wpart[core]

        @pl.loop(0, 15)
        def _(i):
            d = both_ways(i)
            rcopy("wz", r.wpart.at[core], w_mine, d, z, at_z((z + d) % 16)).start()

    r.inv_y[...] = jnp.broadcast_to(prepare(0, r.send_rows[0]), (128, 128))
    prepare_cotangent(0, r.send_rows[1])

    @pl.loop(0, 8)
    def _(i):
        c = 2 * i + p

        @pl.when(c != z)
        def _():
            arrived("wz", r.wb.at[core, c // 8, y, (c % 8) // 2, j], c, at_z(c))

    def w_a(v):
        return r.wb.at[core, 0, y, :, j_of(v)]

    def w_b(v):
        return r.wb.at[core, 1, v, :, j]

    for d in range(1, 4):
        go("wa1", w_a(x), w_a(x), d, x, at_x((x + d) % 4))
        go("wb1", w_b(y), w_b(y), d, y, at_y((y + d) % 4))
    token_sends(0, 3, 8)
    for e in range(2):
        r.p1[e, z_lo, z_hi] = r.send_rows[e, z]

    for d in range(1, 4):
        v = (x + d) % 4
        arrived("wa1", w_a(v), v, at_x(v))
    def half_a(of, v, h):
        return r.wb.at[of, 0, v, 2 * h:2 * h + 2]

    def half_b(of, v, h):
        return r.wb.at[of, 1, 2 * h:2 * h + 2, :, j_of(v)]

    def halves(name, half, v, d, dev):
        for h in range(2):
            go(name, half(core, v, h), half(core, v, h), 2 * d + h, 2 * v + h, dev)

    def hand_on(name, across, half, v, d, dev):
        for h in range(2):
            arrived(name, half(core, v, h), 2 * v + h, dev)
            go(across, half(core, v, h), half(core, v, h), 2 * d + h, 2 * v + h, pair)

    halves("wca", half_a, y, 0, pair)
    for d, span in ((1, (8, 10)), (3, (10, 12)), (2, (12, 15))):
        halves("wa2", half_a, y, d, at_y((y + d) % 4))
        token_sends(0, *span)
    for d in range(1, 4):
        v = (y + d) % 4
        arrived("wb1", w_b(v), v, at_y(v))
    halves("wcb", half_b, x, 0, pair)
    for d, span in ((1, (0, 4)), (3, (4, 8)), (2, (8, 15))):
        halves("wb2", half_b, x, d, at_x((x + d) % 4))
        token_sends(1, *span)

    perm_v = one_hot(
        256, 256, lambda i: (i % 8) * 32 + (i // 128) * 16 + ((i // 8) % 2) * 8 + (i // 16) % 8
    )

    def second_hop(e):
        @pl.loop(1, 16)
        def _(d):
            c = (z + d) % 16
            arrived("p1", r.p1.at[e, c % 8, c // 8], 16 * e + c, at_z(c))

        for d in range(1, 4):
            v = (y + d) % 4
            go("xl", r.p1.at[e, pl.ds(2 * v, 2)], r.xb.at[e, :, y], 4 * e + d, 4 * e + y, at_y(v))
        r.xb[e, :, y] = r.p1[e, pl.ds(2 * y, 2)]
        r.zv[e] = dot(perm_v, r.p1[e].reshape(256, 384)).astype(BF).reshape(8, 2, 16, 384)
        for d in range(1, 8):
            v = (k + d) % 8
            go("zl", r.zv.at[e, v], r.zb.at[e, :, k], 8 * e + d, 8 * e + k, at_k(v))
        r.zb[e, :, k] = r.zv[e, k]

    def lines_arrived(e):
        for d in range(1, 4):
            v = (y + d) % 4
            arrived("xl", r.xb.at[e, :, v], 4 * e + v, at_y(v))
        for d in range(1, 8):
            v = (k + d) % 8
            arrived("zl", r.zb.at[e, :, v], 8 * e + v, at_k(v))

    second_hop(0)

    for d in (1, 3, 2):
        v = (y + d) % 4
        hand_on("wa2", "wca", half_a, v, d, at_y(v))
        v = (x + d) % 4
        hand_on("wb2", "wcb", half_b, v, d, at_x(v))
    def separate(part):
        @pl.loop(0, 2)
        def _(g):
            for e in range(2):
                both = [r.wb[part, g, 2 * e + h].reshape(768, 128).astype(F32) for h in range(2)]
                for h, block in enumerate(swap(*both)):
                    r.wsep[2 * part + h, g, :, e * 128:(e + 1) * 128] = block.astype(BF)

    second_hop(1)
    separate(core)

    for d in range(4):
        v = (y + d) % 4
        for h in range(2):
            arrived("wca", half_a(1 - core, v, h), 2 * v + h, pair)
        v = (x + d) % 4
        for h in range(2):
            arrived("wcb", half_b(1 - core, v, h), 2 * v + h, pair)

    separate(1 - core)

    row_i = lax.broadcasted_iota(jnp.int32, (128, 128), 0)
    col_i = lax.broadcasted_iota(jnp.int32, (128, 128), 1)

    def lines(q, kk, v, u, same):
        lane_head = lax.broadcasted_iota(jnp.int32, (128, 256), 1) // 64

        def spread(a):
            return jnp.concatenate(
                [jnp.where(lane_head == h, a, jnp.zeros_like(a)) for h in range(4)], axis=0
            )

        qs, ks, vs, us = spread(q), spread(kk), spread(v), spread(u)
        s = dot_nt(q, ks)
        dp = dot_nt(u, vs)
        lows, dss = [], []
        for h in range(4):
            sj = jnp.where(same, s[:, h * 128:(h + 1) * 128] * SCALE, -1e30)
            e = jnp.exp(sj - jnp.max(sj, axis=-1, keepdims=True))
            pr = e / jnp.sum(e, axis=-1, keepdims=True)
            dpj = dp[:, h * 128:(h + 1) * 128]
            delta = jnp.sum(pr * dpj, axis=-1, keepdims=True)
            dss.append((pr * (dpj - delta) * SCALE).astype(BF))
            lows.append(pr.astype(BF))
        p_wide, ds_wide = jnp.concatenate(lows, axis=1), jnp.concatenate(dss, axis=1)
        p_tall, ds_tall = jnp.concatenate(lows, axis=0), jnp.concatenate(dss, axis=0)
        return dot(ds_wide, ks), dot_tn(ds_tall, qs), dot_tn(p_tall, us), dot(p_wide, vs)

    def blocks_of(a, b):
        pairs = [swap(a[:, e:e + 128], b[:, e:e + 128]) for e in (0, 128)]
        return jnp.concatenate([*pairs[0], *pairs[1]], axis=1).astype(BF)

    def home(first, count, g, same):
        normed = r.normed[first:first + count].reshape(count * 128, 768)
        c16 = r.c16[first:first + count].reshape(count * 128, 768)
        feats = [dot(normed, r.wsep[c, g]).astype(BF) for c in range(3)]
        feats.append(dot(c16, r.wsep[3, g]).astype(BF))
        grads = [[], [], []]
        for i in range(count):
            here = slice(i * 128, (i + 1) * 128)
            there = slice((first + i) * 128, (first + i + 1) * 128)
            gq, gk, gv, att = lines(*[a[here] for a in feats], same)
            r.gs_qk[g, there, :] = blocks_of(gq, gk)
            r.gs_v[g, there, :] = gv.astype(BF)
            r.gs_a[g, there, :] = att.astype(BF)
            for c, one in enumerate((gq, gk, gv)):
                grads[c].append(one.astype(BF))
        back = [dot_nt(jnp.concatenate(grads[c], axis=0), r.wsep[c, g]) for c in range(3)]
        back = (back[0] + back[1]) + back[2]
        for i in range(count):
            r.gn[first + i] += back[i * 128:(i + 1) * 128]

    @pl.loop(0, 2)
    def _(g):
        home(0, 1, g, row_i % 8 == col_i % 8)

    half = row_i // 64 == col_i // 64
    lines_arrived(0)
    prepare(1, r.xb[0].reshape(16, 16, 384))
    prepare(2, r.zb[0].reshape(16, 16, 384))
    lines_arrived(1)
    prepare_cotangent(1, r.xb[1].reshape(16, 16, 384))
    prepare_cotangent(2, r.zb[1].reshape(16, 16, 384))

    home(1, 2, 0, half)

    def weight_grad(part, g, dest):
        lhs = r.lt[0]
        if part == 0:
            full = dot(lhs, r.gs_qk[g])
            blocks = [full[:, e:e + 128] for e in range(0, 512, 128)]
        else:
            gv, ga = dot(lhs, r.gs_v[g]), dot(r.lt[1], r.gs_a[g])
            blocks = []
            for e in (0, 128):
                blocks.extend(swap(gv[:, e:e + 128], ga[:, e:e + 128]))
        for v in range(4):
            dest[g, v] = blocks[v].astype(dest.dtype)

    def to_other_core(g):
        for part in range(2):
            @pl.when(core == 1 - part)
            def _():
                weight_grad(part, g, r.gw_send)
        go("c", r.gw_send.at[g], r.gw_recv.at[g], g, g, pair)

    def own_part(g):
        for part in range(2):
            @pl.when(core == part)
            def _():
                weight_grad(part, g, r.gw_own)

    def four(ref):
        return (ref[0].astype(F32) + ref[1].astype(F32)) + (ref[2].astype(F32) + ref[3].astype(F32))

    def sum_first(g, between=lambda i: None):
        arrived("c", r.gw_recv.at[g], g, pair)
        for v in range(4):
            both = (r.gw_own[g, v] + r.gw_recv[g, v].astype(F32)).astype(BF).reshape(4, 4, 48, 128)
            r.a1s[g, v] = both[:2]
            for e in range(4):
                r.b1s[g, e, v] = both[2:, e]
        for i, d in enumerate((2, 1, 3)):
            between(i)
            v = (y + d) % 4
            go("a1", r.a1s.at[g, v], r.a1r.at[g, y], 4 * g + d, 4 * g + y, at_y(v))
            v = (x + d) % 4
            go("b1", r.b1s.at[g, j_of(v)], r.b1r.at[g, x], 4 * g + d, 4 * g + x, at_x(v))
        r.a1r[g, y] = r.a1s[g, y]
        r.b1r[g, x] = r.b1s[g, j]

    def sum_second(g):
        for d in range(1, 4):
            v = (y + d) % 4
            arrived("a1", r.a1r.at[g, v], 4 * g + v, at_y(v))
        a_sum = four(r.a1r.at[g]).astype(BF)
        for e in range(4):
            r.a2s[g, e] = a_sum[:, e]
        for d in (2, 1, 3):
            v = (x + d) % 4
            go("a2", r.a2s.at[g, j_of(v)], r.a2r.at[g, x], 4 * g + d, 4 * g + x, at_x(v))
        r.a2r[g, x] = r.a2s[g, j]
        for d in range(1, 4):
            v = (x + d) % 4
            arrived("b1", r.b1r.at[g, v], 4 * g + v, at_x(v))
        r.b2s[g] = four(r.b1r.at[g]).astype(BF)
        for d in (2, 1, 3):
            v = (y + d) % 4
            go("b2", r.b2s.at[g, v], r.b2r.at[g, y], 4 * g + d, 4 * g + y, at_y(v))
        r.b2r[g, y] = r.b2s[g, y]

    def z_copy(g, i):
        c = 8 * g + 2 * i + p
        return rcopy("z", r.zs.at[g, i], r.zr.at[z], 4 * g + i, z, at_z(c))

    def sum_third(g):
        for d in range(1, 4):
            v = (x + d) % 4
            arrived("a2", r.a2r.at[g, v], 4 * g + v, at_x(v))
        r.zs[g, 0:2] = four(r.a2r.at[g]).astype(BF)
        for d in range(1, 4):
            v = (y + d) % 4
            arrived("b2", r.b2r.at[g, v], 4 * g + v, at_y(v))
        r.zs[g, 2:4] = four(r.b2r.at[g]).astype(BF)

        @pl.loop(0, 4)
        def _(i):
            @pl.when(8 * g + 2 * i + p != z)
            def _():
                z_copy(g, i).start()

    home(1, 2, 1, half)

    g = r.gn[1]
    r.gx[...] = g.astype(BF).reshape(2, 4, 16, 768)
    for d in range(1, 4):
        v = (y + d) % 4
        go("gx", r.gx.at[:, v], r.xg.at[pl.ds(2 * y, 2)], d, y, at_y(v))
    r.xg[pl.ds(2 * y, 2)] = r.gx[:, y]
    g4 = r.gn[2].reshape(2, 8, 8, 768)
    r.gz[...] = jnp.concatenate([g4[0], g4[1]], axis=1).astype(BF)
    for d in range(1, 8):
        v = (k + d) % 8
        go("gz", r.gz.at[v], r.zg.at[k], d, k, at_k(v))
    r.zg[k] = r.gz[k]

    parts = [r.gn[0] * r.nrm[0] + r.gn[1] * r.nrm[1] + r.gn[2] * r.nrm[2], r.gn[0] + r.gn[1] + r.gn[2]]
    r.nk[k] = jnp.concatenate([jnp.sum(e, axis=0, keepdims=True) for e in parts], axis=0)
    for d in range(1, 8):
        go("nk", r.nk.at[k], r.nk.at[k], d, k, at_k((k + d) % 8))

    to_other_core(0)
    to_other_core(1)
    own_part(0)
    sum_first(0)
    own_part(1)

    for d in range(1, 8):
        v = (k + d) % 8
        arrived("nk", r.nk.at[v], v, at_k(v))
    both = r.nk[0]
    for v in range(1, 8):
        both = both + r.nk[v]
    r.ny[y] = jnp.where(core == 0, both[0:1], both[1:2])
    for d in range(1, 4):
        go("ny", r.ny.at[y], r.ny.at[y], d, y, at_y((y + d) % 4))

    for d in range(1, 4):
        v = (y + d) % 4
        arrived("gx", r.xg.at[pl.ds(2 * v, 2)], v, at_y(v))
    for d in range(1, 8):
        v = (k + d) % 8
        arrived("gz", r.zg.at[v], v, at_k(v))
    perm_g = one_hot(128, 128, lambda i: (i % 16) * 8 + i // 16)
    total = dot(perm_g, r.zg[...].reshape(128, 768)) + r.xg[...].reshape(128, 768).astype(F32)
    r.rb[...] = fold(total.reshape(16, 8, 768)).astype(BF).reshape(8, 2, 16, 384)

    def return_sends(i):
        @pl.loop(5 * i, 5 * i + 5)
        def _(n):
            d = both_ways(n)
            c = (z + d) % 16
            rcopy("rt", r.rb.at[c % 8, c // 8], r.ret.at[z], d, z, at_z(c)).start()

    for i in range(3):
        return_sends(i)
    sum_first(1)
    for d in range(1, 4):
        v = (y + d) % 4
        arrived("ny", r.ny.at[v], v, at_y(v))
    r.nz[z] = (r.ny[0] + r.ny[1]) + (r.ny[2] + r.ny[3])

    r.ret[z] = r.rb[z_lo, z_hi]

    @pl.loop(0, 15)
    def _(i):
        d = both_ways(i)
        rcopy("nz", r.nz.at[z], r.nz.at[z], d, z, at_z((z + d) % 16)).start()

    sum_second(0)
    sum_second(1)

    sum_third(0)
    sum_third(1)

    @pl.when(holder)
    def _():
        r.zr[z] = r.zs[z_hi, z_lo // 2]

    @pl.loop(1, 16)
    def _(d):
        c = (z + d) % 16
        arrived("rt", r.ret.at[c], c, at_z(c))

    scaled = (r.gn[0] + unfold(r.ret[...])) * gain_row
    nrm = r.nrm[0]
    m1 = jnp.mean(scaled, axis=-1, keepdims=True)
    m2 = jnp.mean(scaled * nrm, axis=-1, keepdims=True)
    c_rows = r.c16[0].astype(F32)
    rows = (c_rows + r.inv_y[:, :1] * (scaled - m1 - nrm * m2)).astype(BF)
    perm_b = one_hot(128, 128, lambda i: (i % 16) * 8 + i // 16)
    r.tok_out[...] = dot(perm_b, rows).astype(BF)
    store_tok = pltpu.make_async_copy(r.tok_out, tok_res, lsem.at[5])
    store_tok.start()

    @pl.loop(1, 16)
    def _(d):
        c = (z + d) % 16
        arrived("nz", r.nz.at[c], c, at_z(c))

    row = r.nz[0]
    for c in range(1, 16):
        row = row + r.nz[c]
    r.norm_out[core] = row
    go("no", r.norm_out.at[core], r.norm_out.at[core], 0, core, pair)

    def final_copies():
        return [rcopy("f", r.qr.at[core], r.qr.at[core], d, core, quad(d)[1]) for d in range(1, 4)]

    @pl.when(holder)
    def _():
        @pl.loop(1, 16)
        def _(d):
            c = (z + d) % 16
            arrived("z", r.zr.at[c], c, at_z(c))

        z_total = r.zr[0].astype(F32)
        for c in range(1, 16):
            z_total = z_total + r.zr[c].astype(F32)
        r.qr[core] = z_total
        for copy in final_copies():
            copy.start()
        arrived("f", r.qr.at[1 - core], 1 - core, pair)

    @pl.when(jnp.logical_not(holder))
    def _():
        for d in range(2):
            arrived("f", r.qr.at[d], d, at_k((x + 1 - 2 * p) * 2 + d))

    arrived("no", r.norm_out.at[1 - core], 1 - core, pair)
    store_norm = pltpu.make_async_copy(r.norm_out, norm_res, lsem.at[6])
    store_norm.start()
    store_w = pltpu.make_async_copy(r.qr, w_res, lsem.at[7])
    store_w.start()

    for copy in sends:
        copy.wait_send()

    @pl.loop(1, 16)
    def _(d):
        c = (z + d) % 16
        dev = at_z(c)
        for e in range(2):
            token_copy(e, d).wait_send()
        rcopy("rt", r.rb.at[c % 8, c // 8], r.ret.at[z], d, z, dev).wait_send()
        rcopy("nz", r.nz.at[z], r.nz.at[z], d, z, dev).wait_send()

    for g in range(2):
        @pl.loop(0, 4)
        def _(i):
            @pl.when(8 * g + 2 * i + p != z)
            def _():
                z_copy(g, i).wait_send()

    @pl.when(holder)
    def _():
        @pl.loop(1, 16)
        def _(d):
            rcopy("wz", r.wpart.at[core], w_mine, d, z, at_z((z + d) % 16)).wait_send()

        for copy in final_copies():
            copy.wait_send()

    store_tok.wait()
    store_norm.wait()
    store_w.wait()


def per_device(tokens, cotangent, weights, norm_gain, norm_bias):
    scratch = list(BUFFERS.values())
    for count in SEMAPHORES.values():
        scratch += [pltpu.SemaphoreType.DMA((count,))] * 2
    scratch.append(pltpu.SemaphoreType.DMA((8,)))
    anywhere = pl.BlockSpec(memory_space=pltpu.HBM)
    grad_tok, grad_w, grad_norm = pl.pallas_call(
        kernel,
        out_shape=(
            jax.ShapeDtypeStruct((128, 768), BF),
            jax.ShapeDtypeStruct((2, 48, 128), F32),
            jax.ShapeDtypeStruct((2, 1, 768), F32),
        ),
        in_specs=[anywhere] * 5,
        out_specs=(anywhere,) * 3,
        scratch_shapes=scratch,
        compiler_params=pltpu.CompilerParams(
            collective_id=0, has_side_effects=True, vmem_limit_bytes=60 * 1024 * 1024
        ),
        name="axial_backward",
    )(tokens.reshape(128, 768), cotangent.reshape(128, 768), weights, norm_gain, norm_bias)
    member = lax.axis_index("slab") % 4
    mine = lax.dynamic_slice(grad_w, (0, member * 12, 0), (2, 12, 128))
    mine = mine.reshape(2, 12, 2, 64).transpose(1, 0, 2, 3).reshape(12, 4, 64)
    return grad_tok.reshape(tokens.shape), mine, grad_norm.reshape(2, 768)


def solution(mesh):
    return jax.shard_map(
        per_device,
        mesh=mesh,
        in_specs=(
            P("slab", "head", None, None),
            P("slab", "head", None, None),
            P("slab", None, "head"),
            P(),
            P(),
        ),
        out_specs=(P("slab", "head", None, None), P("slab", None, "head"), P()),
        check_vma=False,
    )
```
